256 devices in a mesh: dp: 8 (over y_lo, x), owner: 32 (over y_hi, z, core).
Axes of the slice: x: 4, y: 4 (y_hi: 2, y_lo: 2; y = y_hi * 2 + y_lo), z: 8, core: 2. Of those that a mesh axis runs over, the one named last changes fastest.
Arguments:
- gradients: bfloat16 [1024, 14336], P('dp', 'owner'), may hold values from -36 to 36
- activations: bfloat16 [1024, 8192], P('dp', 'owner'), may hold values from -36 to 36
- basis_out: bfloat16 [14336, 14336], P('dp', 'owner'), may hold values from -0.046875 to 0.046875
- basis_in: bfloat16 [8192, 8192], P('dp', 'owner'), may hold values from -0.0625 to 0.0625
Outputs:
- cov_out: float32 [14336, 14336], P('dp', 'owner')
- cov_in: float32 [8192, 8192], P('dp', 'owner')
- corrections: float32 [14336, 8192], P('owner', 'dp')
The draws below stay inside these ranges and needn't reach their ends.
All inputs are finite; a program needn't handle non-finite values.
Results may differ from the reference program's by a relative error of at most 0.00084.
Values may be sent and summed in bfloat16 or wider, within the bound.
A program may use at most 64 MiB of HBM per device.

```python
import math
import jax
import jax.numpy as jnp

DIN = 8192
HID = 14336
TOKENS = 1024


def scale_field(key, base):
    key_rows, key_cols = jax.random.split(key, 2)
    row_scale = jnp.exp(jax.random.uniform(key_rows, (base.shape[0], 1), jnp.float32, math.log(0.3), math.log(3.0)))
    col_scale = jnp.exp(jax.random.uniform(key_cols, (1, base.shape[1]), jnp.float32, math.log(0.3), math.log(3.0)))
    return base * row_scale * col_scale


def draw_gradients(key, part):
    key = jax.random.fold_in(key, 11)
    key_base, key_rest = jax.random.split(key, 2)
    base = jnp.clip(jax.random.normal(key_base, (TOKENS, HID), jnp.float32), -4.0, 4.0)
    return scale_field(key_rest, base).astype(jnp.bfloat16)


def draw_activations(key, part):
    key = jax.random.fold_in(key, 23)
    key_base, key_rest = jax.random.split(key, 2)
    base = jnp.clip(jax.random.normal(key_base, (TOKENS, DIN), jnp.float32), -4.0, 4.0)
    return scale_field(key_rest, base).astype(jnp.bfloat16)


def block_scale(own_key, shape, cuts, low, high):
    def one(axis_at, blocks):
        heights = jax.random.uniform(jax.random.fold_in(jax.random.fold_in(own_key, 6), axis_at), (blocks,), jnp.float32, low / len(cuts), high / len(cuts))
        return jnp.repeat(jnp.exp(heights), shape[axis_at] // blocks).reshape((-1,) + (1,) * (len(shape) - axis_at - 1))

    level = one(*cuts[0])
    for cut in cuts[1:]:
        level = level * one(*cut)
    return level


def gaussian(own_key, dims, spread, bound, cuts=(), kind=jnp.bfloat16):
    array = jax.random.normal(own_key, dims, jnp.float32) * spread
    if len(cuts) > 0:
        array = block_scale(own_key, dims, cuts, -0.22, 0.18) * array
    return jnp.clip(array, min=-bound, max=bound).astype(kind)


def setup_inputs(seed: int = 0) -> dict:
    splits = jax.random.split(jax.random.key(seed), 5)
    gradients = draw_gradients(jax.random.fold_in(splits[4], 71), 0)
    activations = draw_activations(jax.random.fold_in(splits[4], 71), 0)
    basis_out = gaussian(splits[2], (HID, HID), HID ** -0.5, 0.046875, ((0, 8), (1, 32)))
    basis_in = gaussian(splits[3], (DIN, DIN), DIN ** -0.5, 0.0625, ((0, 8), (1, 32)))
    return dict(gradients=gradients, activations=activations, basis_out=basis_out, basis_in=basis_in)


def reference(gradients, activations, basis_out, basis_in):
    cov_out = jnp.dot(gradients.T, gradients, preferred_element_type=jnp.float32) / TOKENS
    cov_in = jnp.dot(activations.T, activations, preferred_element_type=jnp.float32) / TOKENS
    grad_rot = jnp.dot(gradients, basis_out, preferred_element_type=jnp.float32)
    act_rot = jnp.dot(activations, basis_in, preferred_element_type=jnp.float32)
    grad_sq = (grad_rot * grad_rot).astype(jnp.bfloat16)
    act_sq = (act_rot * act_rot).astype(jnp.bfloat16)
    corrections = jnp.dot(grad_sq.T, act_sq, preferred_element_type=jnp.float32) / TOKENS
    return cov_out, cov_in, corrections
```

```python
import jax
import jax.numpy as jnp
from jax import lax
from jax.experimental import pallas as pl
from jax.experimental.pallas import tpu as pltpu
from jax.sharding import PartitionSpec as P

BF16, F32 = jnp.bfloat16, jnp.float32
MESH = pl.DeviceIdType.MESH
GROUPS = 8
CHUNK = 128
GRAD = 448
ACT = 256
BOTH = GRAD + ACT


def dot_nt(left, right):
    return lax.dot_general(
        left, right, (((1,), (1,)), ((), ())), preferred_element_type=F32
    )


def dot_nn(left, right):
    return lax.dot_general(
        left, right, (((1,), (0,)), ((), ())), preferred_element_type=F32
    )


def kernel(
    grad_hbm, act_hbm, bout_hbm, bin_hbm,
    cov_out_hbm, cov_in_hbm, corr_hbm,
    cols, blk, bout, bin_raw, bin_t, act_raw, part, parts_in, mine,
    gsq, asq_own, asq, cov_out, cov_in, corr,
    load_sem, out_sem,
    ent_s, ent_r, up_s, up_r, dn_s, dn_r, sib_s, sib_r,
    ent2_s, ent2_r, up2_s, up2_r, dn2_s, dn2_r, sib2_s, sib2_r,
    col_s, col_r, sum_s, sum_r, gsq_s, gsq_r,
):
    dp, own = lax.axis_index("dp"), lax.axis_index("owner")
    side, z, core = own // 16, (own // 2) % 8, own % 2
    sibling = own + 1 - 2 * core
    up = side * 16 + ((z + 1) % 8) * 2 + core
    down = side * 16 + ((z + 7) % 8) * 2 + core

    def chunk_at(position):
        return (position + 2 * (dp % 4) + 16) % 8

    first = chunk_at(z)
    line = own // 4
    half = z % 2
    entry = (dp + 16 - 2 * (line % 4)) % 8

    def remote(src, dst, send, recv, to):
        return pltpu.make_async_remote_copy(
            src_ref=src, dst_ref=dst, send_sem=send, recv_sem=recv,
            device_id=to, device_id_type=MESH,
        )

    def arrived(ref, recv):
        remote(ref, ref, load_sem.at[0], recv, (dp, sibling)).wait_recv()

    def sent(ref, send):
        remote(ref, ref, send, load_sem.at[0], (dp, sibling)).wait_send()

    loads = [
        pltpu.make_async_copy(act_hbm, act_raw, load_sem.at[0]),
        pltpu.make_async_copy(grad_hbm, cols.at[dp, pl.ds(0, GRAD)], load_sem.at[1]),
        pltpu.make_async_copy(bin_hbm, bin_raw, load_sem.at[2]),
        pltpu.make_async_copy(bout_hbm, bout, load_sem.at[3]),
    ]
    for load in loads:
        load.start()

    barrier = pltpu.get_barrier_semaphore()

    def greet(to):
        pl.semaphore_signal(barrier, inc=1, device_id=to, device_id_type=MESH)

    @pl.loop(1, GROUPS)
    def _(i):
        greet(((dp + i) % 8, own))

    greet((dp, sibling))
    greet((dp, up))
    greet((dp, down))
    for j in range(2):
        source = 4 * dp + 2 * j + core

        @pl.when(jnp.logical_or(first != dp, source != own))
        def _():
            greet((first, source))

    loads[0].wait()
    cols[dp, GRAD:, :] = act_raw[...].T
    loads[1].wait()
    at_home = jnp.logical_and(line == dp, entry == z)
    pl.semaphore_wait(barrier, 12 - jnp.where(at_home, 1, 0))

    def enter(src, dst, send, recv):
        for j in range(2):
            target = j * 16 + entry * 2 + core
            local = jnp.logical_and(line == dp, target == own)

            @pl.when(local)
            def _():
                copy = pltpu.make_async_copy(src, dst, recv.at[half])
                copy.start()

            @pl.when(jnp.logical_not(local))
            def _():
                remote(src, dst, send.at[j], recv.at[half], (line, target)).start()

    def entered(src, send):
        for j in range(2):
            target = j * 16 + entry * 2 + core
            local = jnp.logical_and(line == dp, target == own)

            @pl.when(jnp.logical_not(local))
            def _():
                sent(src, send.at[j])

    def ring(buf, ent_r, up_s, up_r, dn_s, dn_r, sib_s, sib_r, between):
        def share(index, ref):
            remote(ref, ref, sib_s.at[index], sib_r.at[index], (dp, sibling)).start()

        def forward(step, ref_up, ref_down):
            if ref_up is not None:
                remote(ref_up, ref_up, up_s.at[step], up_r.at[step], (dp, up)).start()
            if ref_down is not None:
                remote(ref_down, ref_down, dn_s.at[step], dn_r.at[step], (dp, down)).start()

        for j in range(2):
            arrived(buf.at[first, core, j], ent_r.at[j])
        unit = buf.at[first, core]
        forward(0, unit, unit)
        share(0, unit)
        between(0)
        for step in range(1, 5):
            below, above = chunk_at(z - step), chunk_at(z + step)
            if step < 4:
                unit = buf.at[below, core]
                arrived(unit, up_r.at[step - 1])
                forward(step, unit if step < 3 else buf.at[below, core, 0], None)
                share(2 * step - 1, unit)
                unit = buf.at[above, core]
                arrived(unit, dn_r.at[step - 1])
                forward(step, None, unit if step < 3 else buf.at[above, core, 1])
                share(2 * step, unit)
            else:
                arrived(buf.at[above, core, 0], up_r.at[3])
                share(7, buf.at[above, core, 0])
                arrived(buf.at[above, core, 1], dn_r.at[3])
                share(8, buf.at[above, core, 1])
            between(step)

    def shared(buf, sib_r, step):
        other = 1 - core
        if step == 0:
            arrived(buf.at[first, other], sib_r.at[0])
        elif step < 4:
            arrived(buf.at[chunk_at(z - step), other], sib_r.at[2 * step - 1])
            arrived(buf.at[chunk_at(z + step), other], sib_r.at[2 * step])
        else:
            arrived(buf.at[chunk_at(z + 4), other, 0], sib_r.at[7])
            arrived(buf.at[chunk_at(z + 4), other, 1], sib_r.at[8])

    def ring_sent(buf, up_s, dn_s, sib_s):
        for step in range(4):
            if step < 3:
                sent(buf.at[first, core], up_s.at[step])
                sent(buf.at[first, core], dn_s.at[step])
            else:
                sent(buf.at[first, core, 0], up_s.at[step])
                sent(buf.at[first, core, 1], dn_s.at[step])
        for index in range(7):
            sent(buf.at[first, core], sib_s.at[index])
        for index in (7, 8):
            sent(buf.at[first, core, 0], sib_s.at[index])

    def rotate(t):
        grads = jnp.concatenate(
            [blk[t, c, j, :GRAD, :] for j in range(2) for c in range(2)], axis=0
        )
        acts = jnp.concatenate(
            [blk[t, c, j, GRAD:, :] for j in range(2) for c in range(2)], axis=0
        )
        part[t, :GRAD, :] = dot_nn(bout[...], grads)
        part[t, GRAD:, :] = dot_nn(bin_t[...], acts)

        @pl.when(t != dp)
        def _():
            remote(part.at[t], parts_in.at[dp], sum_s.at[t], sum_r.at[dp], (t, own)).start()

    def rotations(step):
        shared(blk, sib_r, step)
        if step == 0:
            rotate(first)
        elif step < 4:

            @pl.loop(0, 2)
            def _(i):
                rotate(chunk_at(z + (2 * i - 1) * step))
        else:
            rotate(chunk_at(z + 4))

    def beside_first(step):
        if step == 0:

            @pl.loop(1, GROUPS)
            def _(i):
                peer = (dp + i) % 8
                remote(cols.at[dp], cols.at[dp], col_s.at[peer], col_r.at[dp], (peer, own)).start()

            loads[2].wait()
            bin_t[...] = bin_raw[...].T
            loads[3].wait()
        else:
            rotations(step - 1)

    enter(cols.at[dp], blk.at[dp, core, half], ent_s, ent_r)
    ring(blk, ent_r, up_s, up_r, dn_s, dn_r, sib_s, sib_r, beside_first)
    rotations(4)

    mine[...] = part[dp]

    @pl.loop(1, GROUPS)
    def _(i):
        source = (dp + i) % 8
        arrived(parts_in.at[source], sum_r.at[source])
        mine[...] += parts_in[source]

    squares = (mine[...] * mine[...]).astype(BF16)
    gsq[dp] = squares[:GRAD]
    asq_own[...] = squares[GRAD:]
    enter(asq_own, asq.at[dp, core, half], ent2_s, ent2_r)

    @pl.loop(1, GROUPS)
    def _(i):
        peer = (dp + i) % 8
        remote(gsq.at[dp], gsq.at[dp], gsq_s.at[peer], gsq_r.at[dp], (peer, own)).start()

    def tokens(ref, *index):
        return jnp.concatenate([ref[(t,) + index] for t in range(GROUPS)], axis=1)

    grad_rows, act_rows = pl.ds(0, GRAD), pl.ds(GRAD, ACT)
    scale = 1.0 / (GROUPS * CHUNK)

    def beside_second(step):
        if step == 0:

            @pl.loop(1, GROUPS)
            def _(i):
                source = (dp + i) % 8
                arrived(cols.at[source], col_r.at[source])

        elif step < 3:
            j = step - 1
            rows = jnp.concatenate([tokens(blk, c, j, grad_rows) for c in range(2)], axis=0)
            cov_out[:, 2 * GRAD * j : 2 * GRAD * (j + 1)] = (
                dot_nt(tokens(cols, grad_rows), rows) * scale
            )
            if step == 2:
                pltpu.make_async_copy(cov_out, cov_out_hbm, out_sem.at[0]).start()
        elif step == 3:
            rows = jnp.concatenate(
                [tokens(blk, c, j, act_rows) for j in range(2) for c in range(2)], axis=0
            )
            cov_in[...] = dot_nt(rows, tokens(cols, act_rows)) * scale
            pltpu.make_async_copy(cov_in, cov_in_hbm, out_sem.at[1]).start()

    ring(asq, ent2_r, up2_s, up2_r, dn2_s, dn2_r, sib2_s, sib2_r, beside_second)

    @pl.loop(1, GROUPS)
    def _(i):
        source = (dp + i) % 8
        arrived(gsq.at[source], gsq_r.at[source])

    for step in range(5):
        shared(asq, sib2_r, step)
    rows = jnp.concatenate([tokens(asq, c, j) for j in range(2) for c in range(2)], axis=0)
    corr[...] = dot_nt(tokens(gsq), rows) * scale
    last = pltpu.make_async_copy(corr, corr_hbm, out_sem.at[2])
    last.start()

    entered(cols.at[dp], ent_s)
    entered(asq_own, ent2_s)
    ring_sent(blk, up_s, dn_s, sib_s)
    ring_sent(asq, up2_s, dn2_s, sib2_s)

    @pl.loop(1, GROUPS)
    def _(i):
        peer = (dp + i) % 8
        sent(cols.at[dp], col_s.at[peer])
        sent(part.at[peer], sum_s.at[peer])
        sent(gsq.at[dp], gsq_s.at[peer])

    pltpu.make_async_copy(cov_out, cov_out_hbm, out_sem.at[0]).wait()
    pltpu.make_async_copy(cov_in, cov_in_hbm, out_sem.at[1]).wait()
    last.wait()


def on_device(gradients, activations, basis_out, basis_in):
    dma = pltpu.SemaphoreType.DMA
    ring_sems = [dma((2,)), dma((2,))] + [dma((4,))] * 4 + [dma((9,))] * 2
    cov_out_t, cov_in, corrections = pl.pallas_call(
        kernel,
        out_shape=(
            jax.ShapeDtypeStruct((GRAD, 4 * GRAD), F32),
            jax.ShapeDtypeStruct((4 * ACT, ACT), F32),
            jax.ShapeDtypeStruct((GRAD, 4 * ACT), F32),
        ),
        in_specs=[pl.BlockSpec(memory_space=pl.ANY)] * 4,
        out_specs=[pl.BlockSpec(memory_space=pl.ANY)] * 3,
        scratch_shapes=[
            pltpu.VMEM((GROUPS, BOTH, CHUNK), BF16),
            pltpu.VMEM((GROUPS, 2, 2, BOTH, CHUNK), BF16),
            pltpu.VMEM((GRAD, 4 * GRAD), BF16),
            pltpu.VMEM((4 * ACT, ACT), BF16),
            pltpu.VMEM((ACT, 4 * ACT), BF16),
            pltpu.VMEM((CHUNK, ACT), BF16),
            pltpu.VMEM((GROUPS, BOTH, CHUNK), F32),
            pltpu.VMEM((GROUPS, BOTH, CHUNK), F32),
            pltpu.VMEM((BOTH, CHUNK), F32),
            pltpu.VMEM((GROUPS, GRAD, CHUNK), BF16),
            pltpu.VMEM((ACT, CHUNK), BF16),
            pltpu.VMEM((GROUPS, 2, 2, ACT, CHUNK), BF16),
            pltpu.VMEM((GRAD, 4 * GRAD), F32),
            pltpu.VMEM((4 * ACT, ACT), F32),
            pltpu.VMEM((GRAD, 4 * ACT), F32),
            dma((4,)),
            dma((3,)),
            *ring_sems,
            *ring_sems,
            *[dma((GROUPS,))] * 6,
        ],
        compiler_params=pltpu.CompilerParams(
            collective_id=0, has_side_effects=True, vmem_limit_bytes=52 << 20
        ),
    )(gradients.T, activations, basis_out.T, basis_in)
    return cov_out_t.T, cov_in, corrections


def solution(mesh):
    placed = (P("dp", "owner"), P("dp", "owner"), P("dp", "owner"), P("dp", "owner"))
    return jax.shard_map(
        on_device,
        mesh=mesh,
        in_specs=placed,
        out_specs=(P("dp", "owner"), P("dp", "owner"), P("owner", "dp")),
        check_vma=False,
    )
```

```python
import jax
import jax.numpy as jnp
from jax import lax
from jax.experimental import pallas as pl
from jax.experimental.pallas import tpu as pltpu
from jax.sharding import PartitionSpec as P

BF16, F32 = jnp.bfloat16, jnp.float32
MESH = pl.DeviceIdType.MESH
GROUPS = 8
CHUNK = 128
GRAD = 448
ACT = 256
BOTH = GRAD + ACT
SCALES = 16
SPAN = 240.0


def dot_nt(left, right):
    return lax.dot_general(
        left, right, (((1,), (1,)), ((), ())), preferred_element_type=F32
    )


def dot_nn(left, right):
    return lax.dot_general(
        left, right, (((1,), (0,)), ((), ())), preferred_element_type=F32
    )


def encode(values):
    largest = jnp.max(jnp.abs(values), axis=0, keepdims=True)
    scale = jnp.maximum(largest * 1.0079, 1e-30).astype(BF16).astype(F32)
    code = jnp.exp2(jnp.abs(values) * (SPAN / scale) - SPAN / 2)
    return jnp.where(values < 0, -code, code).astype(BF16), scale


def decode(code, scale):
    code = code.astype(F32)
    values = (jnp.log2(jnp.abs(code)) + SPAN / 2) * (scale * (1 / SPAN))
    return jnp.where(code < 0, -values, values)


def kernel(
    grad_hbm, act_hbm, bout_hbm, bin_hbm,
    cov_out, cov_in, gsq, asq,
    cols, blk, bout, bin_raw, bin_t, act_raw, rot, part, parts_in, mine, total, asq_own,
    load_sem,
    ent_s, ent_r, up_s, up_r, dn_s, dn_r, sib_s, sib_r,
    ent2_s, ent2_r, up2_s, up2_r, dn2_s, dn2_r, sib2_s, sib2_r,
    col_s, col_r, sum_s, sum_r, gsq_s, gsq_r,
):
    dp, own = lax.axis_index("dp"), lax.axis_index("owner")
    side, z, core = own // 16, (own // 2) % 8, own % 2
    sibling = own + 1 - 2 * core
    up = side * 16 + ((z + 1) % 8) * 2 + core
    down = side * 16 + ((z + 7) % 8) * 2 + core

    def chunk_at(position):
        return (position + 2 * (dp % 4) + 16) % 8

    first = chunk_at(z)
    line = own // 4
    half = z % 2
    entry = (dp + 16 - 2 * (line % 4)) % 8

    def remote(src, dst, send, recv, to):
        return pltpu.make_async_remote_copy(
            src_ref=src, dst_ref=dst, send_sem=send, recv_sem=recv,
            device_id=to, device_id_type=MESH,
        )

    def arrived(ref, recv):
        remote(ref, ref, load_sem.at[0], recv, (dp, sibling)).wait_recv()

    def sent(ref, send):
        remote(ref, ref, send, load_sem.at[0], (dp, sibling)).wait_send()

    loads = [
        pltpu.make_async_copy(act_hbm, act_raw, load_sem.at[0]),
        pltpu.make_async_copy(grad_hbm, cols.at[dp, pl.ds(0, GRAD)], load_sem.at[1]),
        pltpu.make_async_copy(bin_hbm, bin_raw, load_sem.at[2]),
        pltpu.make_async_copy(bout_hbm, bout, load_sem.at[3]),
    ]
    for load in loads:
        load.start()

    barrier = pltpu.get_barrier_semaphore()

    def greet(to):
        pl.semaphore_signal(barrier, inc=1, device_id=to, device_id_type=MESH)

    @pl.loop(1, GROUPS)
    def _(i):
        greet(((dp + i) % 8, own))

    greet((dp, sibling))
    greet((dp, up))
    greet((dp, down))
    for j in range(2):
        source = 4 * dp + 2 * j + core

        @pl.when(jnp.logical_or(first != dp, source != own))
        def _():
            greet((first, source))

    loads[0].wait()
    cols[dp, GRAD:, :] = act_raw[...].T
    loads[1].wait()
    at_home = jnp.logical_and(line == dp, entry == z)
    pl.semaphore_wait(barrier, 12 - jnp.where(at_home, 1, 0))

    def enter(src, dst, send, recv):
        for j in range(2):
            target = j * 16 + entry * 2 + core
            local = jnp.logical_and(line == dp, target == own)

            @pl.when(local)
            def _():
                pltpu.make_async_copy(src, dst, recv.at[half]).start()

            @pl.when(jnp.logical_not(local))
            def _():
                remote(src, dst, send.at[j], recv.at[half], (line, target)).start()

    def entered(src, send):
        for j in range(2):
            target = j * 16 + entry * 2 + core
            local = jnp.logical_and(line == dp, target == own)

            @pl.when(jnp.logical_not(local))
            def _():
                sent(src, send.at[j])

    def ring(buf, ent_r, up_s, up_r, dn_s, dn_r, sib_s, sib_r, between):
        def share(index, j, ref):
            remote(
                ref, ref, sib_s.at[index, j], sib_r.at[index, j], (dp, sibling)
            ).start()

        def to_up(step, j, ref):
            remote(ref, ref, up_s.at[step, j], up_r.at[step, j], (dp, up)).start()

        def to_down(step, j, ref):
            remote(ref, ref, dn_s.at[step, j], dn_r.at[step, j], (dp, down)).start()

        for j in range(2):
            piece = buf.at[first, core, j]
            arrived(piece, ent_r.at[j])
            to_up(0, j, piece)
            to_down(0, j, piece)
            share(0, j, piece)
            between(0, j)
        for step in range(1, 5):
            below, above = chunk_at(z - step), chunk_at(z + step)
            for j in range(2):
                if step < 4 or j == 0:
                    piece = buf.at[below, core, j]
                    arrived(piece, up_r.at[step - 1, j])
                    if step < 3 or (step == 3 and j == 0):
                        to_up(step, j, piece)
                    share(2 * step - 1, j, piece)
                if step < 4 or j == 1:
                    piece = buf.at[above, core, j]
                    arrived(piece, dn_r.at[step - 1, j])
                    if step < 3 or (step == 3 and j == 1):
                        to_down(step, j, piece)
                    share(2 * step if step < 4 else 7, j, piece)
                between(step, j)

    def shared(buf, sib_r, index):
        step = (index + 1) // 2
        chunk = chunk_at(z - step if index % 2 else z + step)
        for j in range(2):
            arrived(buf.at[chunk, 1 - core, j], sib_r.at[index, j])
        return chunk

    def ring_sent(buf, up_s, dn_s, sib_s):
        piece = buf.at[first, core, 0]
        for step in range(4):
            for j in range(2):
                if step < 3 or j == 0:
                    sent(piece, up_s.at[step, j])
                if step < 3 or j == 1:
                    sent(piece, dn_s.at[step, j])
        for index in range(8):
            for j in range(2):
                sent(piece, sib_s.at[index, j])

    def rotate(index):
        t = shared(blk, sib_r, index)
        grads = jnp.concatenate(
            [blk[t, c, j, :GRAD, :] for j in range(2) for c in range(2)], axis=0
        )
        acts = jnp.concatenate(
            [blk[t, c, j, GRAD:, :] for j in range(2) for c in range(2)], axis=0
        )
        rot[:GRAD, :] = dot_nn(bout[...], grads)
        rot[GRAD:, :] = dot_nn(bin_t[...], acts)

        @pl.when(t == dp)
        def _():
            mine[...] = rot[...]

        @pl.when(t != dp)
        def _():
            code, grad_scale = encode(rot[:GRAD, :])
            part[t, :GRAD, :] = code
            code, act_scale = encode(rot[GRAD:, :])
            part[t, GRAD:BOTH, :] = code
            part[t, BOTH:, :] = jnp.concatenate(
                [
                    jnp.broadcast_to(grad_scale, (SCALES // 2, CHUNK)),
                    jnp.broadcast_to(act_scale, (SCALES // 2, CHUNK)),
                ],
                axis=0,
            ).astype(BF16)
            remote(part.at[t], parts_in.at[dp], sum_s.at[t], sum_r.at[dp], (t, own)).start()

    def send_columns(low, high):
        @pl.loop(low, high)
        def _(i):
            peer = (dp + i) % 8
            remote(
                cols.at[dp], cols.at[dp], col_s.at[peer], col_r.at[dp], (peer, own)
            ).start()

    def add_parts(order):
        for g in order:

            @pl.loop(0, 2)
            def _(i):
                source = i * 4 + (((dp - z + 8) % 8) // 2 + g) % 4

                @pl.when(source != dp)
                def _():
                    arrived(parts_in.at[source], sum_r.at[source])
                    scales = parts_in[source, BOTH:, :].astype(F32)
                    total[:GRAD, :] += decode(parts_in[source, :GRAD, :], scales[:1])
                    total[GRAD:, :] += decode(
                        parts_in[source, GRAD:BOTH, :], scales[SCALES // 2 : SCALES // 2 + 1]
                    )

    def beside_first(step, j):
        if step == 0:
            if j == 1:
                send_columns(1, 3)
                bin_t[...] = bin_raw[...].T
                total[...] = jnp.zeros_like(total)
        elif step == 1:
            if j == 0:
                loads[3].wait()
                rotate(0)
            else:
                send_columns(3, 5)
        else:
            rotate(2 * step - 3 + j)
            if step < 4 and j == 1:
                send_columns(2 * step + 1, min(2 * step + 3, GROUPS))
            if step == 4 and j == 0:
                add_parts((0,))

    enter(cols.at[dp], blk.at[dp, core, half], ent_s, ent_r)
    loads[2].wait()
    ring(blk, ent_r, up_s, up_r, dn_s, dn_r, sib_s, sib_r, beside_first)
    rotate(7)
    add_parts((1,))

    def tokens(ref, *index):
        return jnp.concatenate([ref[(t,) + index] for t in range(GROUPS)], axis=1)

    grad_rows, act_rows = pl.ds(0, GRAD), pl.ds(GRAD, ACT)
    scale = 1.0 / (GROUPS * CHUNK)

    def covariance_out(j):
        rows = jnp.concatenate([tokens(blk, c, j, grad_rows) for c in range(2)], axis=0)
        cov_out[:, 2 * GRAD * j : 2 * GRAD * (j + 1)] = (
            dot_nt(tokens(cols, grad_rows), rows) * scale
        )

    @pl.loop(1, GROUPS)
    def _(i):
        source = (dp + i) % 8
        arrived(cols.at[source], col_r.at[source])

    covariance_out(0)
    add_parts((3, 2))

    sums = total[...] + mine[...]
    squares = (sums * sums).astype(BF16)
    asq_own[...] = squares[GRAD:]
    enter(asq_own, asq.at[dp, core, half], ent2_s, ent2_r)
    gsq[dp] = squares[:GRAD]

    @pl.loop(1, GROUPS)
    def _(i):
        peer = (dp + i) % 8
        remote(gsq.at[dp], gsq.at[dp], gsq_s.at[peer], gsq_r.at[dp], (peer, own)).start()

    covariance_out(1)

    def beside_second(step, j):
        if (step, j) == (0, 1):
            rows = jnp.concatenate(
                [tokens(blk, c, j, act_rows) for j in range(2) for c in range(2)], axis=0
            )
            cov_in[...] = dot_nt(rows, tokens(cols, act_rows)) * scale
        if (step, j) == (2, 0):
            entered(cols.at[dp], ent_s)
            ring_sent(blk, up_s, dn_s, sib_s)

            @pl.loop(1, GROUPS)
            def _(i):
                peer = (dp + i) % 8
                sent(cols.at[dp], col_s.at[peer])
                sent(part.at[peer], sum_s.at[peer])

    ring(asq, ent2_r, up2_s, up2_r, dn2_s, dn2_r, sib2_s, sib2_r, beside_second)

    @pl.loop(1, GROUPS)
    def _(i):
        source, peer = (dp + i) % 8, (dp + i) % 8
        arrived(gsq.at[source], gsq_r.at[source])
        sent(gsq.at[dp], gsq_s.at[peer])

    for index in range(8):
        shared(asq, sib2_r, index)
    entered(asq_own, ent2_s)
    ring_sent(asq, up2_s, dn2_s, sib2_s)


def finish(cov_out, cov_in, gsq, asq, cov_out_hbm, cov_in_hbm, corr_hbm, corr, sem):
    first = pltpu.make_async_copy(cov_out, cov_out_hbm, sem.at[0])
    second = pltpu.make_async_copy(cov_in, cov_in_hbm, sem.at[1])
    first.start()
    second.start()
    left = jnp.concatenate([gsq[t] for t in range(GROUPS)], axis=1)
    for j in range(2):
        right = jnp.concatenate(
            [
                jnp.concatenate([asq[t, c, j] for t in range(GROUPS)], axis=1)
                for c in range(2)
            ],
            axis=0,
        )
        columns = slice(2 * ACT * j, 2 * ACT * (j + 1))
        corr[:, columns] = dot_nt(left, right) * (1.0 / (GROUPS * CHUNK))
    last = pltpu.make_async_copy(corr, corr_hbm, sem.at[2])
    last.start()
    first.wait()
    second.wait()
    last.wait()


def on_device(gradients, activations, basis_out, basis_in):
    dma = pltpu.SemaphoreType.DMA
    ring_sems = [dma((2,)), dma((2,))] + [dma((4, 2))] * 4 + [dma((8, 2))] * 2
    inputs = [
        pltpu.with_memory_space_constraint(x, pltpu.HBM)
        for x in (gradients.T, activations, basis_out.T, basis_in)
    ]
    results = pl.pallas_call(
        kernel,
        out_shape=(
            pltpu.VMEM((GRAD, 4 * GRAD), F32),
            pltpu.VMEM((4 * ACT, ACT), F32),
            pltpu.VMEM((GROUPS, GRAD, CHUNK), BF16),
            pltpu.VMEM((GROUPS, 2, 2, ACT, CHUNK), BF16),
        ),
        in_specs=[pl.BlockSpec(memory_space=pl.ANY)] * 4,
        out_specs=[pl.BlockSpec(memory_space=pltpu.VMEM)] * 4,
        scratch_shapes=[
            pltpu.VMEM((GROUPS, BOTH, CHUNK), BF16),
            pltpu.VMEM((GROUPS, 2, 2, BOTH, CHUNK), BF16),
            pltpu.VMEM((GRAD, 4 * GRAD), BF16),
            pltpu.VMEM((4 * ACT, ACT), BF16),
            pltpu.VMEM((ACT, 4 * ACT), BF16),
            pltpu.VMEM((CHUNK, ACT), BF16),
            pltpu.VMEM((BOTH, CHUNK), F32),
            pltpu.VMEM((GROUPS, BOTH + SCALES, CHUNK), BF16),
            pltpu.VMEM((GROUPS, BOTH + SCALES, CHUNK), BF16),
            pltpu.VMEM((BOTH, CHUNK), F32),
            pltpu.VMEM((BOTH, CHUNK), F32),
            pltpu.VMEM((ACT, CHUNK), BF16),
            dma((4,)),
            *ring_sems,
            *ring_sems,
            *[dma((GROUPS,))] * 6,
        ],
        compiler_params=pltpu.CompilerParams(
            collective_id=0, has_side_effects=True, vmem_limit_bytes=36 << 20
        ),
    )(*inputs)
    results = [pltpu.with_memory_space_constraint(x, pltpu.VMEM) for x in results]
    cov_out_t, cov_in, corrections = pl.pallas_call(
        finish,
        out_shape=(
            jax.ShapeDtypeStruct((GRAD, 4 * GRAD), F32),
            jax.ShapeDtypeStruct((4 * ACT, ACT), F32),
            jax.ShapeDtypeStruct((GRAD, 4 * ACT), F32),
        ),
        in_specs=[pl.BlockSpec(memory_space=pltpu.VMEM)] * 4,
        out_specs=[pl.BlockSpec(memory_space=pl.ANY)] * 3,
        scratch_shapes=[pltpu.VMEM((GRAD, 4 * ACT), F32), dma((3,))],
        compiler_params=pltpu.CompilerParams(vmem_limit_bytes=36 << 20),
    )(*results)
    return cov_out_t.T, cov_in, corrections


def solution(mesh):
    placed = (P("dp", "owner"), P("dp", "owner"), P("dp", "owner"), P("dp", "owner"))
    return jax.shard_map(
        on_device,
        mesh=mesh,
        in_specs=placed,
        out_specs=(P("dp", "owner"), P("dp", "owner"), P("owner", "dp")),
        check_vma=False,
    )
```

```python
import jax
import jax.numpy as jnp
from jax import lax
from jax.experimental import pallas as pl
from jax.experimental.pallas import tpu as pltpu
from jax.sharding import PartitionSpec as P

BF16, F32 = jnp.bfloat16, jnp.float32
MESH = pl.DeviceIdType.MESH
GROUPS = 8
CHUNK = 128
GRAD = 448
ACT = 256
BOTH = GRAD + ACT
SCALES = 16
SPAN = 240.0


def dot_nt(left, right):
    return lax.dot_general(
        left, right, (((1,), (1,)), ((), ())), preferred_element_type=F32
    )


def dot_nn(left, right):
    return lax.dot_general(
        left, right, (((1,), (0,)), ((), ())), preferred_element_type=F32
    )


def encode(values):
    largest = jnp.max(jnp.abs(values), axis=0, keepdims=True)
    scale = jnp.maximum(largest * 1.0079, 1e-30).astype(BF16).astype(F32)
    code = jnp.exp2(jnp.abs(values) * (SPAN / scale) - SPAN / 2)
    return jnp.where(values < 0, -code, code).astype(BF16), scale


def decode(code, scale):
    code = code.astype(F32)
    values = (jnp.log2(jnp.abs(code)) + SPAN / 2) * (scale * (1 / SPAN))
    return jnp.where(code < 0, -values, values)


def kernel(
    grad_hbm, act_hbm, bout_hbm, bin_hbm,
    cov_out, cov_in, gsq, asq,
    cols, blk, bout, bin_raw, bin_t, act_raw, rot, part, parts_in, mine, total, asq_own,
    load_sem,
    ent_s, ent_r, up_s, up_r, dn_s, dn_r, sib_s, sib_r,
    ent2_s, ent2_r, up2_s, up2_r, dn2_s, dn2_r, sib2_s, sib2_r,
    col_s, col_r, sum_s, sum_r, gsq_s, gsq_r,
):
    dp, own = lax.axis_index("dp"), lax.axis_index("owner")
    side, z, core = own // 16, (own // 2) % 8, own % 2
    sibling = own + 1 - 2 * core
    up = side * 16 + ((z + 1) % 8) * 2 + core
    down = side * 16 + ((z + 7) % 8) * 2 + core

    def chunk_at(position):
        return (4 * side + 16 - position - dp % 4) % 8

    first = chunk_at(z)
    line = own // 4
    half = z % 2

    def entry(ring):
        return (4 * ring + 16 - dp - line % 4) % 8


    def remote(src, dst, send, recv, to):
        return pltpu.make_async_remote_copy(
            src_ref=src, dst_ref=dst, send_sem=send, recv_sem=recv,
            device_id=to, device_id_type=MESH,
        )

    def arrived(ref, recv):
        remote(ref, ref, load_sem.at[0], recv, (dp, sibling)).wait_recv()

    def sent(ref, send):
        remote(ref, ref, send, load_sem.at[0], (dp, sibling)).wait_send()

    loads = [
        pltpu.make_async_copy(act_hbm, act_raw, load_sem.at[0]),
        pltpu.make_async_copy(grad_hbm, cols.at[dp, pl.ds(0, GRAD)], load_sem.at[1]),
        pltpu.make_async_copy(bin_hbm, bin_raw, load_sem.at[2]),
        pltpu.make_async_copy(bout_hbm, bout, load_sem.at[3]),
    ]
    for load in loads:
        load.start()

    barrier = pltpu.get_barrier_semaphore()

    def greet(to):
        pl.semaphore_signal(barrier, inc=1, device_id=to, device_id_type=MESH)

    @pl.loop(1, GROUPS)
    def _(i):
        greet(((dp + i) % 8, own))

    greet((dp, sibling))
    greet((dp, up))
    greet((dp, down))
    for j in range(2):
        source = 4 * dp + 2 * j + core

        @pl.when(jnp.logical_or(first != dp, source != own))
        def _():
            greet((first, source))

    loads[0].wait()
    cols[dp, GRAD:, :] = act_raw[...].T
    loads[1].wait()
    at_home = jnp.logical_and(line == dp, entry(side) == z)
    pl.semaphore_wait(barrier, 12 - jnp.where(at_home, 1, 0))

    def enter(src, dst, send, recv):
        for j in range(2):
            target = j * 16 + entry(j) * 2 + core
            local = jnp.logical_and(line == dp, target == own)

            @pl.when(local)
            def _():
                pltpu.make_async_copy(src, dst, recv.at[half]).start()

            @pl.when(jnp.logical_not(local))
            def _():
                remote(src, dst, send.at[j], recv.at[half], (line, target)).start()

    def entered(src, send):
        for j in range(2):
            target = j * 16 + entry(j) * 2 + core
            local = jnp.logical_and(line == dp, target == own)

            @pl.when(jnp.logical_not(local))
            def _():
                sent(src, send.at[j])

    def ring(buf, ent_r, up_s, up_r, dn_s, dn_r, sib_s, sib_r, between):
        def share(index, j, ref):
            remote(
                ref, ref, sib_s.at[index, j], sib_r.at[index, j], (dp, sibling)
            ).start()

        def to_up(step, j, ref):
            remote(ref, ref, up_s.at[step, j], up_r.at[step, j], (dp, up)).start()

        def to_down(step, j, ref):
            remote(ref, ref, dn_s.at[step, j], dn_r.at[step, j], (dp, down)).start()

        for j in range(2):
            piece = buf.at[first, core, j]
            arrived(piece, ent_r.at[j])
            to_up(0, j, piece)
            to_down(0, j, piece)
            share(0, j, piece)
            between(0, j)
        for step in range(1, 5):
            below, above = chunk_at(z - step), chunk_at(z + step)
            for j in range(2):
                if step < 4 or j == 0:
                    piece = buf.at[below, core, j]
                    arrived(piece, up_r.at[step - 1, j])
                    if step < 3 or (step == 3 and j == 0):
                        to_up(step, j, piece)
                    share(2 * step - 1, j, piece)
                if step < 4 or j == 1:
                    piece = buf.at[above, core, j]
                    arrived(piece, dn_r.at[step - 1, j])
                    if step < 3 or (step == 3 and j == 1):
                        to_down(step, j, piece)
                    share(2 * step if step < 4 else 7, j, piece)
                between(step, j)

    def shared(buf, sib_r, index):
        step = (index + 1) // 2
        chunk = chunk_at(z - step if index % 2 else z + step)
        for j in range(2):
            arrived(buf.at[chunk, 1 - core, j], sib_r.at[index, j])
        return chunk

    def ring_sent(buf, up_s, dn_s, sib_s):
        piece = buf.at[first, core, 0]
        for step in range(4):
            for j in range(2):
                if step < 3 or j == 0:
                    sent(piece, up_s.at[step, j])
                if step < 3 or j == 1:
                    sent(piece, dn_s.at[step, j])
        for index in range(8):
            for j in range(2):
                sent(piece, sib_s.at[index, j])

    def rotate(index):
        t = shared(blk, sib_r, index)
        grads = jnp.concatenate(
            [blk[t, c, j, :GRAD, :] for j in range(2) for c in range(2)], axis=0
        )
        acts = jnp.concatenate(
            [blk[t, c, j, GRAD:, :] for j in range(2) for c in range(2)], axis=0
        )
        rot[:GRAD, :] = dot_nn(bout[...], grads)
        rot[GRAD:, :] = dot_nn(bin_t[...], acts)

        @pl.when(t == dp)
        def _():
            mine[...] = rot[...]

        @pl.when(t != dp)
        def _():
            code, grad_scale = encode(rot[:GRAD, :])
            part[t, :GRAD, :] = code
            code, act_scale = encode(rot[GRAD:, :])
            part[t, GRAD:BOTH, :] = code
            part[t, BOTH:, :] = jnp.concatenate(
                [
                    jnp.broadcast_to(grad_scale, (SCALES // 2, CHUNK)),
                    jnp.broadcast_to(act_scale, (SCALES // 2, CHUNK)),
                ],
                axis=0,
            ).astype(BF16)
            remote(part.at[t], parts_in.at[dp], sum_s.at[t], sum_r.at[dp], (t, own)).start()

    def send_columns(low, high):
        @pl.loop(low, high)
        def _(i):
            peer = (dp + i) % 8
            remote(
                cols.at[dp], cols.at[dp], col_s.at[peer], col_r.at[dp], (peer, own)
            ).start()

    def add_parts(low, high):
        @pl.loop(2 * low, 2 * high)
        def _(i):
            turn = i // 2
            steps = (turn + 1) // 2 * (1 - 2 * (turn % 2))
            column = (4 * side + 24 - dp - z - steps) % 8
            source = i % 2 * 4 + column

            @pl.when(jnp.logical_and(column < 4, source != dp))
            def _():
                arrived(parts_in.at[source], sum_r.at[source])
                scales = parts_in[source, BOTH:, :].astype(F32)
                total[:GRAD, :] += decode(parts_in[source, :GRAD, :], scales[:1])
                total[GRAD:, :] += decode(
                    parts_in[source, GRAD:BOTH, :], scales[SCALES // 2 : SCALES // 2 + 1]
                )

    def beside_first(step, j):
        if step == 0:
            if j == 1:
                send_columns(1, GROUPS)
                bin_t[...] = bin_raw[...].T
                total[...] = jnp.zeros_like(total)
        elif step == 1:
            if j == 0:
                loads[3].wait()
                rotate(0)
        else:
            rotate(2 * step - 3 + j)
            if step == 4 and j == 0:
                add_parts(0, 3)

    enter(cols.at[dp], blk.at[dp, core, half], ent_s, ent_r)
    loads[2].wait()
    ring(blk, ent_r, up_s, up_r, dn_s, dn_r, sib_s, sib_r, beside_first)
    rotate(7)
    add_parts(3, 5)

    def tokens(ref, *index):
        return jnp.concatenate([ref[(t,) + index] for t in range(GROUPS)], axis=1)

    grad_rows, act_rows = pl.ds(0, GRAD), pl.ds(GRAD, ACT)
    scale = 1.0 / (GROUPS * CHUNK)

    def covariance_out(j):
        rows = jnp.concatenate([tokens(blk, c, j, grad_rows) for c in range(2)], axis=0)
        cov_out[:, 2 * GRAD * j : 2 * GRAD * (j + 1)] = (
            dot_nt(tokens(cols, grad_rows), rows) * scale
        )

    @pl.loop(1, GROUPS)
    def _(i):
        source = (dp + i) % 8
        arrived(cols.at[source], col_r.at[source])

    covariance_out(0)
    add_parts(5, 8)

    sums = total[...] + mine[...]
    squares = (sums * sums).astype(BF16)
    asq_own[...] = squares[GRAD:]
    enter(asq_own, asq.at[dp, core, half], ent2_s, ent2_r)
    gsq[dp] = squares[:GRAD]

    covariance_out(1)

    def beside_second(step, j):
        if (step, j) == (0, 1):

            @pl.loop(1, GROUPS)
            def _(i):
                peer = (dp + i) % 8
                remote(
                    gsq.at[dp], gsq.at[dp], gsq_s.at[peer], gsq_r.at[dp], (peer, own)
                ).start()

            rows = jnp.concatenate(
                [tokens(blk, c, j, act_rows) for j in range(2) for c in range(2)], axis=0
            )
            cov_in[...] = dot_nt(rows, tokens(cols, act_rows)) * scale
        if (step, j) == (2, 0):
            entered(cols.at[dp], ent_s)
            ring_sent(blk, up_s, dn_s, sib_s)

            @pl.loop(1, GROUPS)
            def _(i):
                peer = (dp + i) % 8
                sent(cols.at[dp], col_s.at[peer])
                sent(part.at[peer], sum_s.at[peer])

    ring(asq, ent2_r, up2_s, up2_r, dn2_s, dn2_r, sib2_s, sib2_r, beside_second)

    @pl.loop(1, GROUPS)
    def _(i):
        source, peer = (dp + i) % 8, (dp + i) % 8
        arrived(gsq.at[source], gsq_r.at[source])
        sent(gsq.at[dp], gsq_s.at[peer])

    for index in range(8):
        shared(asq, sib2_r, index)
    entered(asq_own, ent2_s)
    ring_sent(asq, up2_s, dn2_s, sib2_s)


def finish(cov_out, cov_in, gsq, asq, cov_out_hbm, cov_in_hbm, corr_hbm, corr, sem):
    first = pltpu.make_async_copy(cov_out, cov_out_hbm, sem.at[0])
    second = pltpu.make_async_copy(cov_in, cov_in_hbm, sem.at[1])
    first.start()
    second.start()
    left = jnp.concatenate([gsq[t] for t in range(GROUPS)], axis=1)
    for j in range(2):
        right = jnp.concatenate(
            [
                jnp.concatenate([asq[t, c, j] for t in range(GROUPS)], axis=1)
                for c in range(2)
            ],
            axis=0,
        )
        columns = slice(2 * ACT * j, 2 * ACT * (j + 1))
        corr[:, columns] = dot_nt(left, right) * (1.0 / (GROUPS * CHUNK))
    last = pltpu.make_async_copy(corr, corr_hbm, sem.at[2])
    last.start()
    first.wait()
    second.wait()
    last.wait()


def on_device(gradients, activations, basis_out, basis_in):
    dma = pltpu.SemaphoreType.DMA
    ring_sems = [dma((2,)), dma((2,))] + [dma((4, 2))] * 4 + [dma((8, 2))] * 2
    inputs = [
        pltpu.with_memory_space_constraint(x, pltpu.HBM)
        for x in (gradients.T, activations, basis_out.T, basis_in)
    ]
    results = pl.pallas_call(
        kernel,
        out_shape=(
            pltpu.VMEM((GRAD, 4 * GRAD), F32),
            pltpu.VMEM((4 * ACT, ACT), F32),
            pltpu.VMEM((GROUPS, GRAD, CHUNK), BF16),
            pltpu.VMEM((GROUPS, 2, 2, ACT, CHUNK), BF16),
        ),
        in_specs=[pl.BlockSpec(memory_space=pl.ANY)] * 4,
        out_specs=[pl.BlockSpec(memory_space=pltpu.VMEM)] * 4,
        scratch_shapes=[
            pltpu.VMEM((GROUPS, BOTH, CHUNK), BF16),
            pltpu.VMEM((GROUPS, 2, 2, BOTH, CHUNK), BF16),
            pltpu.VMEM((GRAD, 4 * GRAD), BF16),
            pltpu.VMEM((4 * ACT, ACT), BF16),
            pltpu.VMEM((ACT, 4 * ACT), BF16),
            pltpu.VMEM((CHUNK, ACT), BF16),
            pltpu.VMEM((BOTH, CHUNK), F32),
            pltpu.VMEM((GROUPS, BOTH + SCALES, CHUNK), BF16),
            pltpu.VMEM((GROUPS, BOTH + SCALES, CHUNK), BF16),
            pltpu.VMEM((BOTH, CHUNK), F32),
            pltpu.VMEM((BOTH, CHUNK), F32),
            pltpu.VMEM((ACT, CHUNK), BF16),
            dma((4,)),
            *ring_sems,
            *ring_sems,
            *[dma((GROUPS,))] * 6,
        ],
        compiler_params=pltpu.CompilerParams(
            collective_id=0, has_side_effects=True, vmem_limit_bytes=36 << 20
        ),
    )(*inputs)
    results = [pltpu.with_memory_space_constraint(x, pltpu.VMEM) for x in results]
    cov_out_t, cov_in, corrections = pl.pallas_call(
        finish,
        out_shape=(
            jax.ShapeDtypeStruct((GRAD, 4 * GRAD), F32),
            jax.ShapeDtypeStruct((4 * ACT, ACT), F32),
            jax.ShapeDtypeStruct((GRAD, 4 * ACT), F32),
        ),
        in_specs=[pl.BlockSpec(memory_space=pltpu.VMEM)] * 4,
        out_specs=[pl.BlockSpec(memory_space=pl.ANY)] * 3,
        scratch_shapes=[pltpu.VMEM((GRAD, 4 * ACT), F32), dma((3,))],
        compiler_params=pltpu.CompilerParams(vmem_limit_bytes=36 << 20),
    )(*results)
    return cov_out_t.T, cov_in, corrections


def solution(mesh):
    placed = (P("dp", "owner"), P("dp", "owner"), P("dp", "owner"), P("dp", "owner"))
    return jax.shard_map(
        on_device,
        mesh=mesh,
        in_specs=placed,
        out_specs=(P("dp", "owner"), P("dp", "owner"), P("owner", "dp")),
        check_vma=False,
    )
```

```python
import jax
import jax.numpy as jnp
from jax import lax
from jax.experimental import pallas as pl
from jax.experimental.pallas import tpu as pltpu
from jax.sharding import PartitionSpec as P

BF16, F32 = jnp.bfloat16, jnp.float32
MESH = pl.DeviceIdType.MESH
GROUPS = 8
CHUNK = 128
GRAD = 448
ACT = 256
BOTH = GRAD + ACT
SCALES = 16
SPAN = 240.0


def dot_nt(left, right):
    return lax.dot_general(
        left, right, (((1,), (1,)), ((), ())), preferred_element_type=F32
    )


def dot_nn(left, right):
    return lax.dot_general(
        left, right, (((1,), (0,)), ((), ())), preferred_element_type=F32
    )


def encode(values):
    largest = jnp.max(jnp.abs(values), axis=0, keepdims=True)
    scale = jnp.maximum(largest * 1.0079, 1e-30).astype(BF16).astype(F32)
    code = jnp.exp2(jnp.abs(values) * (SPAN / scale) - SPAN / 2)
    return jnp.where(values < 0, -code, code).astype(BF16), scale


def decode(code, scale):
    code = code.astype(F32)
    values = (jnp.log2(jnp.abs(code)) + SPAN / 2) * (scale * (1 / SPAN))
    return jnp.where(code < 0, -values, values)


def kernel(
    grad_hbm, act_hbm, bout_hbm, bin_hbm,
    cov_out, cov_in, gsq, asq,
    cols, blk, bout, bin_raw, bin_t, act_raw, rot, part, parts_in, mine, total, asq_own,
    load_sem,
    ent_s, ent_r, x_s, x_r, up_s, up_r, dn_s, dn_r, sib_s, sib_r,
    ent2_s, ent2_r, x2_s, x2_r, up2_s, up2_r, dn2_s, dn2_r, sib2_s, sib2_r,
    col_s, col_r, sum_s, sum_r, gsq_s, gsq_r,
):
    dp, own = lax.axis_index("dp"), lax.axis_index("owner")
    side, z, core = own // 16, (own // 2) % 8, own % 2
    sibling = own + 1 - 2 * core
    across = (own + 16) % 32
    up = side * 16 + ((z + 1) % 8) * 2 + core
    down = side * 16 + ((z + 7) % 8) * 2 + core

    def chunk_at(position):
        return (4 * side + 16 - position - dp % 4) % 8

    first = chunk_at(z)
    line = own // 4
    half = z % 2

    def entry(ring):
        return (4 * ring + 16 - dp - line % 4) % 8


    def remote(src, dst, send, recv, to):
        return pltpu.make_async_remote_copy(
            src_ref=src, dst_ref=dst, send_sem=send, recv_sem=recv,
            device_id=to, device_id_type=MESH,
        )

    def arrived(ref, recv):
        remote(ref, ref, load_sem.at[0], recv, (dp, sibling)).wait_recv()

    def sent(ref, send):
        remote(ref, ref, send, load_sem.at[0], (dp, sibling)).wait_send()

    loads = [
        pltpu.make_async_copy(act_hbm, act_raw, load_sem.at[0]),
        pltpu.make_async_copy(grad_hbm, cols.at[dp, pl.ds(0, GRAD)], load_sem.at[1]),
        pltpu.make_async_copy(bin_hbm, bin_raw, load_sem.at[2]),
        pltpu.make_async_copy(bout_hbm, bout, load_sem.at[3]),
    ]
    for load in loads:
        load.start()

    barrier = pltpu.get_barrier_semaphore()

    def greet(to):
        pl.semaphore_signal(barrier, inc=1, device_id=to, device_id_type=MESH)

    @pl.loop(1, GROUPS)
    def _(i):
        greet(((dp + i) % 8, own))

    greet((dp, sibling))
    greet((dp, across))
    greet((dp, up))
    greet((dp, down))
    for j in range(2):
        source = 4 * dp + 2 * j + core

        @pl.when(jnp.logical_or(first != dp, source != own))
        def _():
            greet((first, source))

    loads[0].wait()
    cols[dp, GRAD:, :] = act_raw[...].T
    loads[1].wait()
    at_home = jnp.logical_and(line == dp, entry(side) == z)
    pl.semaphore_wait(barrier, 13 - jnp.where(at_home, 1, 0))

    def enter(src, dst, send, recv):
        for j in range(2):
            target = j * 16 + entry(j) * 2 + core
            local = jnp.logical_and(line == dp, target == own)

            @pl.when(local)
            def _():
                pltpu.make_async_copy(src, dst, recv.at[half]).start()

            @pl.when(jnp.logical_not(local))
            def _():
                remote(src, dst, send.at[j], recv.at[half], (line, target)).start()

    def entered(src, send):
        for j in range(2):
            target = j * 16 + entry(j) * 2 + core
            local = jnp.logical_and(line == dp, target == own)

            @pl.when(jnp.logical_not(local))
            def _():
                sent(src, send.at[j])

    def ring(buf, ent_r, x_s, x_r, up_s, up_r, dn_s, dn_r, sib_s, sib_r, between):
        def share(index, j, ref):
            remote(
                ref, ref, sib_s.at[index, j], sib_r.at[index, j], (dp, sibling)
            ).start()

        def to_up(step, j, ref):
            remote(ref, ref, up_s.at[step, j], up_r.at[step, j], (dp, up)).start()

        def to_down(step, j, ref):
            remote(ref, ref, dn_s.at[step, j], dn_r.at[step, j], (dp, down)).start()

        for j in range(2):
            piece = buf.at[first, core, j]
            arrived(piece, ent_r.at[j])
            to_up(0, j, piece)
            to_down(0, j, piece)
            remote(piece, piece, x_s.at[j], x_r.at[j], (dp, across)).start()
            share(0, j, piece)
            between(0, j)
        for step in range(1, 4):
            below, above = chunk_at(z - step), chunk_at(z + step)
            for j in range(2):
                piece = buf.at[below, core, j]
                arrived(piece, up_r.at[step - 1, j])
                if step < 3:
                    to_up(step, j, piece)
                share(2 * step - 1, j, piece)
                piece = buf.at[above, core, j]
                arrived(piece, dn_r.at[step - 1, j])
                if step < 3:
                    to_down(step, j, piece)
                share(2 * step, j, piece)
                if step == 2:
                    piece = buf.at[chunk_at(z + 4), core, j]
                    arrived(piece, x_r.at[j])
                    share(7, j, piece)
                between(step, j)

    def shared(buf, sib_r, index):
        step = (index + 1) // 2
        chunk = chunk_at(z - step if index % 2 else z + step)
        for j in range(2):
            arrived(buf.at[chunk, 1 - core, j], sib_r.at[index, j])
        return chunk

    def ring_sent(buf, x_s, up_s, dn_s, sib_s):
        piece = buf.at[first, core, 0]
        for j in range(2):
            sent(piece, x_s.at[j])
            for step in range(3):
                sent(piece, up_s.at[step, j])
                sent(piece, dn_s.at[step, j])
            for index in range(8):
                sent(piece, sib_s.at[index, j])

    def rotate(index):
        t = shared(blk, sib_r, index)
        grads = jnp.concatenate(
            [blk[t, c, j, :GRAD, :] for j in range(2) for c in range(2)], axis=0
        )
        acts = jnp.concatenate(
            [blk[t, c, j, GRAD:, :] for j in range(2) for c in range(2)], axis=0
        )
        rot[:GRAD, :] = dot_nn(bout[...], grads)
        rot[GRAD:, :] = dot_nn(bin_t[...], acts)

        @pl.when(t == dp)
        def _():
            mine[...] = rot[...]

        @pl.when(t != dp)
        def _():
            code, grad_scale = encode(rot[:GRAD, :])
            part[t, :GRAD, :] = code
            code, act_scale = encode(rot[GRAD:, :])
            part[t, GRAD:BOTH, :] = code
            part[t, BOTH:, :] = jnp.concatenate(
                [
                    jnp.broadcast_to(grad_scale, (SCALES // 2, CHUNK)),
                    jnp.broadcast_to(act_scale, (SCALES // 2, CHUNK)),
                ],
                axis=0,
            ).astype(BF16)
            remote(part.at[t], parts_in.at[dp], sum_s.at[t], sum_r.at[dp], (t, own)).start()

    opposite = (dp + 4) % 8

    def column_copy(chunk, index, peer):
        return remote(
            cols.at[chunk], cols.at[chunk], col_s.at[index], col_r.at[chunk], (peer, own)
        )

    def send_columns():
        arrived(cols.at[opposite], col_r.at[opposite])

        @pl.loop(1, 4)
        def _(i):
            peer = dp // 4 * 4 + (dp + i) % 4
            column_copy(dp, peer, peer).start()
            column_copy(opposite, (peer + 4) % 8, peer).start()

    def add_parts(low, high):
        @pl.loop(2 * low, 2 * high)
        def _(i):
            turn = i // 2
            steps = (turn + 1) // 2 * (1 - 2 * (turn % 2))
            column = (4 * side + 24 - dp - z - steps) % 8
            source = i % 2 * 4 + column

            @pl.when(jnp.logical_and(column < 4, source != dp))
            def _():
                arrived(parts_in.at[source], sum_r.at[source])
                scales = parts_in[source, BOTH:, :].astype(F32)
                total[:GRAD, :] += decode(parts_in[source, :GRAD, :], scales[:1])
                total[GRAD:, :] += decode(
                    parts_in[source, GRAD:BOTH, :], scales[SCALES // 2 : SCALES // 2 + 1]
                )

    def beside_first(step, j):
        if step == 0:
            if j == 1:
                send_columns()
                bin_t[...] = bin_raw[...].T
                total[...] = jnp.zeros_like(total)
                loads[3].wait()
                rotate(0)
        elif j == 1:
            rotate(2 * step - 1)
            rotate(2 * step)
        elif step == 3:
            rotate(7)
            add_parts(0, 3)

    enter(cols.at[dp], blk.at[dp, core, half], ent_s, ent_r)
    column_copy(dp, opposite, opposite).start()
    loads[2].wait()
    ring(blk, ent_r, x_s, x_r, up_s, up_r, dn_s, dn_r, sib_s, sib_r, beside_first)
    add_parts(3, 5)

    def tokens(ref, *index):
        return jnp.concatenate([ref[(t,) + index] for t in range(GROUPS)], axis=1)

    grad_rows, act_rows = pl.ds(0, GRAD), pl.ds(GRAD, ACT)
    scale = 1.0 / (GROUPS * CHUNK)

    def covariance_out(j):
        rows = jnp.concatenate([tokens(blk, c, j, grad_rows) for c in range(2)], axis=0)
        cov_out[:, 2 * GRAD * j : 2 * GRAD * (j + 1)] = (
            dot_nt(tokens(cols, grad_rows), rows) * scale
        )

    @pl.loop(1, GROUPS)
    def _(i):
        source = (dp + i) % 8

        @pl.when(source != opposite)
        def _():
            arrived(cols.at[source], col_r.at[source])

    covariance_out(0)
    add_parts(5, 8)

    sums = total[...] + mine[...]
    squares = (sums * sums).astype(BF16)
    asq_own[...] = squares[GRAD:]
    enter(asq_own, asq.at[dp, core, half], ent2_s, ent2_r)
    gsq[dp] = squares[:GRAD]

    covariance_out(1)

    def beside_second(step, j):
        if (step, j) == (0, 1):

            @pl.loop(1, GROUPS)
            def _(i):
                peer = (dp + i) % 8
                remote(
                    gsq.at[dp], gsq.at[dp], gsq_s.at[peer], gsq_r.at[dp], (peer, own)
                ).start()

            rows = jnp.concatenate(
                [tokens(blk, c, j, act_rows) for j in range(2) for c in range(2)], axis=0
            )
            cov_in[...] = dot_nt(rows, tokens(cols, act_rows)) * scale
        if (step, j) == (2, 0):
            entered(cols.at[dp], ent_s)
            ring_sent(blk, x_s, up_s, dn_s, sib_s)

            @pl.loop(1, GROUPS)
            def _(i):
                peer = (dp + i) % 8
                sent(cols.at[dp], col_s.at[peer])
                sent(part.at[peer], sum_s.at[peer])

    ring(asq, ent2_r, x2_s, x2_r, up2_s, up2_r, dn2_s, dn2_r, sib2_s, sib2_r, beside_second)

    @pl.loop(1, GROUPS)
    def _(i):
        source, peer = (dp + i) % 8, (dp + i) % 8
        arrived(gsq.at[source], gsq_r.at[source])
        sent(gsq.at[dp], gsq_s.at[peer])

    for index in range(8):
        shared(asq, sib2_r, index)
    entered(asq_own, ent2_s)
    ring_sent(asq, x2_s, up2_s, dn2_s, sib2_s)


def finish(cov_out, cov_in, gsq, asq, cov_out_hbm, cov_in_hbm, corr_hbm, corr, sem):
    first = pltpu.make_async_copy(cov_out, cov_out_hbm, sem.at[0])
    second = pltpu.make_async_copy(cov_in, cov_in_hbm, sem.at[1])
    first.start()
    second.start()
    left = jnp.concatenate([gsq[t] for t in range(GROUPS)], axis=1)
    for j in range(2):
        right = jnp.concatenate(
            [
                jnp.concatenate([asq[t, c, j] for t in range(GROUPS)], axis=1)
                for c in range(2)
            ],
            axis=0,
        )
        columns = slice(2 * ACT * j, 2 * ACT * (j + 1))
        corr[:, columns] = dot_nt(left, right) * (1.0 / (GROUPS * CHUNK))
    last = pltpu.make_async_copy(corr, corr_hbm, sem.at[2])
    last.start()
    first.wait()
    second.wait()
    last.wait()


def on_device(gradients, activations, basis_out, basis_in):
    dma = pltpu.SemaphoreType.DMA
    ring_sems = [dma((2,))] * 4 + [dma((3, 2))] * 4 + [dma((8, 2))] * 2
    inputs = [
        pltpu.with_memory_space_constraint(x, pltpu.HBM)
        for x in (gradients.T, activations, basis_out.T, basis_in)
    ]
    results = pl.pallas_call(
        kernel,
        out_shape=(
            pltpu.VMEM((GRAD, 4 * GRAD), F32),
            pltpu.VMEM((4 * ACT, ACT), F32),
            pltpu.VMEM((GROUPS, GRAD, CHUNK), BF16),
            pltpu.VMEM((GROUPS, 2, 2, ACT, CHUNK), BF16),
        ),
        in_specs=[pl.BlockSpec(memory_space=pl.ANY)] * 4,
        out_specs=[pl.BlockSpec(memory_space=pltpu.VMEM)] * 4,
        scratch_shapes=[
            pltpu.VMEM((GROUPS, BOTH, CHUNK), BF16),
            pltpu.VMEM((GROUPS, 2, 2, BOTH, CHUNK), BF16),
            pltpu.VMEM((GRAD, 4 * GRAD), BF16),
            pltpu.VMEM((4 * ACT, ACT), BF16),
            pltpu.VMEM((ACT, 4 * ACT), BF16),
            pltpu.VMEM((CHUNK, ACT), BF16),
            pltpu.VMEM((BOTH, CHUNK), F32),
            pltpu.VMEM((GROUPS, BOTH + SCALES, CHUNK), BF16),
            pltpu.VMEM((GROUPS, BOTH + SCALES, CHUNK), BF16),
            pltpu.VMEM((BOTH, CHUNK), F32),
            pltpu.VMEM((BOTH, CHUNK), F32),
            pltpu.VMEM((ACT, CHUNK), BF16),
            dma((4,)),
            *ring_sems,
            *ring_sems,
            *[dma((GROUPS,))] * 6,
        ],
        compiler_params=pltpu.CompilerParams(
            collective_id=0, has_side_effects=True, vmem_limit_bytes=36 << 20
        ),
    )(*inputs)
    results = [pltpu.with_memory_space_constraint(x, pltpu.VMEM) for x in results]
    cov_out_t, cov_in, corrections = pl.pallas_call(
        finish,
        out_shape=(
            jax.ShapeDtypeStruct((GRAD, 4 * GRAD), F32),
            jax.ShapeDtypeStruct((4 * ACT, ACT), F32),
            jax.ShapeDtypeStruct((GRAD, 4 * ACT), F32),
        ),
        in_specs=[pl.BlockSpec(memory_space=pltpu.VMEM)] * 4,
        out_specs=[pl.BlockSpec(memory_space=pl.ANY)] * 3,
        scratch_shapes=[pltpu.VMEM((GRAD, 4 * ACT), F32), dma((3,))],
        compiler_params=pltpu.CompilerParams(vmem_limit_bytes=36 << 20),
    )(*results)
    return cov_out_t.T, cov_in, corrections


def solution(mesh):
    placed = (P("dp", "owner"), P("dp", "owner"), P("dp", "owner"), P("dp", "owner"))
    return jax.shard_map(
        on_device,
        mesh=mesh,
        in_specs=placed,
        out_specs=(P("dp", "owner"), P("dp", "owner"), P("owner", "dp")),
        check_vma=False,
    )
```

```python
import jax
import jax.numpy as jnp
from jax import lax
from jax.experimental import pallas as pl
from jax.experimental.pallas import tpu as pltpu
from jax.sharding import PartitionSpec as P

BF16, F32 = jnp.bfloat16, jnp.float32
MESH = pl.DeviceIdType.MESH
GROUPS = 8
CHUNK = 128
GRAD = 448
ACT = 256
BOTH = GRAD + ACT
SCALES = 16
SPAN = 240.0


def dot_nt(left, right):
    return lax.dot_general(
        left, right, (((1,), (1,)), ((), ())), preferred_element_type=F32
    )


def dot_nn(left, right):
    return lax.dot_general(
        left, right, (((1,), (0,)), ((), ())), preferred_element_type=F32
    )


def encode(values):
    largest = jnp.max(jnp.abs(values), axis=0, keepdims=True)
    scale = jnp.maximum(largest * 1.0079, 1e-30).astype(BF16).astype(F32)
    code = jnp.exp2(jnp.abs(values) * (SPAN / scale) - SPAN / 2)
    return jnp.where(values < 0, -code, code).astype(BF16), scale


def decode(code, scale):
    code = code.astype(F32)
    values = (jnp.log2(jnp.abs(code)) + SPAN / 2) * (scale * (1 / SPAN))
    return jnp.where(code < 0, -values, values)


def kernel(
    grad_hbm, act_hbm, bout_hbm, bin_hbm,
    cov_out, cov_in, gsq, asq,
    cols, blk_g, blk_a, bout, bin_raw, bin_t, act_raw, rot, part_g, part_a, in_g, in_a,
    mine, total, asq_own, load_sem, *sems,
):
    ring_g, ring_a, ring_q = sems[:10], sems[10:20], sems[20:30]
    col_s, col_r, sum_gs, sum_gr, sum_as, sum_ar, gsq_s, gsq_r = sems[30:]
    dp, own = lax.axis_index("dp"), lax.axis_index("owner")
    side, z, core = own // 16, (own // 2) % 8, own % 2
    sibling = own + 1 - 2 * core
    across = (own + 16) % 32
    up = side * 16 + ((z + 1) % 8) * 2 + core
    down = side * 16 + ((z + 7) % 8) * 2 + core

    def chunk_at(position):
        return (4 * side + 16 - position - dp % 4) % 8

    first = chunk_at(z)
    line = own // 4
    half = z % 2

    def entry(ring):
        return (4 * ring + 16 - dp - line % 4) % 8


    def remote(src, dst, send, recv, to):
        return pltpu.make_async_remote_copy(
            src_ref=src, dst_ref=dst, send_sem=send, recv_sem=recv,
            device_id=to, device_id_type=MESH,
        )

    def arrived(ref, recv):
        remote(ref, ref, load_sem.at[0], recv, (dp, sibling)).wait_recv()

    def sent(ref, send):
        remote(ref, ref, send, load_sem.at[0], (dp, sibling)).wait_send()

    loads = [
        pltpu.make_async_copy(act_hbm, act_raw, load_sem.at[0]),
        pltpu.make_async_copy(grad_hbm, cols.at[dp, pl.ds(0, GRAD)], load_sem.at[1]),
        pltpu.make_async_copy(bin_hbm, bin_raw, load_sem.at[2]),
        pltpu.make_async_copy(bout_hbm, bout, load_sem.at[3]),
    ]
    for load in loads:
        load.start()

    barrier = pltpu.get_barrier_semaphore()

    def greet(to):
        pl.semaphore_signal(barrier, inc=1, device_id=to, device_id_type=MESH)

    @pl.loop(1, GROUPS)
    def _(i):
        greet(((dp + i) % 8, own))

    greet((dp, sibling))
    greet((dp, across))
    greet((dp, up))
    greet((dp, down))
    for j in range(2):
        source = 4 * dp + 2 * j + core

        @pl.when(jnp.logical_or(first != dp, source != own))
        def _():
            greet((first, source))

    loads[0].wait()
    cols[dp, GRAD:, :] = act_raw[...].T
    loads[1].wait()
    at_home = jnp.logical_and(line == dp, entry(side) == z)
    pl.semaphore_wait(barrier, 13 - jnp.where(at_home, 1, 0))

    def enter(src, dst, send, recv):
        for j in range(2):
            target = j * 16 + entry(j) * 2 + core
            local = jnp.logical_and(line == dp, target == own)

            @pl.when(local)
            def _():
                pltpu.make_async_copy(src, dst, recv.at[half]).start()

            @pl.when(jnp.logical_not(local))
            def _():
                remote(src, dst, send.at[j], recv.at[half], (line, target)).start()

    def entered(src, send):
        for j in range(2):
            target = j * 16 + entry(j) * 2 + core
            local = jnp.logical_and(line == dp, target == own)

            @pl.when(jnp.logical_not(local))
            def _():
                sent(src, send.at[j])

    def ring_copies(buf, ring):
        ent_s, ent_r, x_s, x_r, up_s, up_r, dn_s, dn_r, sib_s, sib_r = ring

        def share(index, j, ref):
            remote(
                ref, ref, sib_s.at[index, j], sib_r.at[index, j], (dp, sibling)
            ).start()

        def to_up(step, j, ref):
            remote(ref, ref, up_s.at[step, j], up_r.at[step, j], (dp, up)).start()

        def to_down(step, j, ref):
            remote(ref, ref, dn_s.at[step, j], dn_r.at[step, j], (dp, down)).start()

        return share, to_up, to_down

    def ring_start(buf, ring):
        share, to_up, to_down = ring_copies(buf, ring)
        for j in range(2):
            piece = buf.at[first, core, j]
            arrived(piece, ring[1].at[j])
            to_up(0, j, piece)
            to_down(0, j, piece)
            remote(piece, piece, ring[2].at[j], ring[3].at[j], (dp, across)).start()
            share(0, j, piece)

    def ring_rest(buf, ring, between):
        share, to_up, to_down = ring_copies(buf, ring)
        for step in range(1, 4):
            below, above = chunk_at(z - step), chunk_at(z + step)
            for j in range(2):
                piece = buf.at[below, core, j]
                arrived(piece, ring[5].at[step - 1, j])
                if step < 3:
                    to_up(step, j, piece)
                share(2 * step - 1, j, piece)
                piece = buf.at[above, core, j]
                arrived(piece, ring[7].at[step - 1, j])
                if step < 3:
                    to_down(step, j, piece)
                share(2 * step, j, piece)
                if step == 2:
                    piece = buf.at[chunk_at(z + 4), core, j]
                    arrived(piece, ring[3].at[j])
                    share(7, j, piece)
                between(step, j)

    def shared(buf, ring, index):
        step = (index + 1) // 2
        chunk = chunk_at(z - step if index % 2 else z + step)
        for j in range(2):
            arrived(buf.at[chunk, 1 - core, j], ring[9].at[index, j])
        return chunk

    def ring_sent(buf, ring):
        piece = buf.at[first, core, 0]
        for j in range(2):
            sent(piece, ring[2].at[j])
            for step in range(3):
                sent(piece, ring[4].at[step, j])
                sent(piece, ring[6].at[step, j])
            for index in range(8):
                sent(piece, ring[8].at[index, j])

    def rotate(index, buf, ring, basis, rows, part, parts_in, sum_s, sum_r):
        t = shared(buf, ring, index)
        features = jnp.concatenate(
            [buf[t, c, j] for j in range(2) for c in range(2)], axis=0
        )
        rot[rows, :] = dot_nn(basis[...], features)
        height = rows.stop - rows.start

        @pl.when(t == dp)
        def _():
            mine[rows, :] = rot[rows, :]

        @pl.when(t != dp)
        def _():
            code, largest = encode(rot[rows, :])
            part[t, :height, :] = code
            part[t, height:, :] = jnp.broadcast_to(largest, (SCALES, CHUNK)).astype(BF16)
            remote(part.at[t], parts_in.at[dp], sum_s.at[t], sum_r.at[dp], (t, own)).start()

    def rotate_g(index):
        rotate(index, blk_g, ring_g, bout, slice(0, GRAD), part_g, in_g, sum_gs, sum_gr)

    def rotate_a(index):
        rotate(index, blk_a, ring_a, bin_t, slice(GRAD, BOTH), part_a, in_a, sum_as, sum_ar)

    opposite = (dp + 4) % 8

    def column_copy(chunk, index, peer):
        return remote(
            cols.at[chunk], cols.at[chunk], col_s.at[index], col_r.at[chunk], (peer, own)
        )

    def send_columns():
        arrived(cols.at[opposite], col_r.at[opposite])

        @pl.loop(1, 4)
        def _(i):
            peer = dp // 4 * 4 + (dp + i) % 4
            column_copy(dp, peer, peer).start()
            column_copy(opposite, (peer + 4) % 8, peer).start()

    def add_parts(rows, parts_in, sum_r):
        height = rows.stop - rows.start

        @pl.loop(0, 16)
        def _(i):
            turn = i // 2
            steps = (turn + 1) // 2 * (1 - 2 * (turn % 2))
            column = (4 * side + 24 - dp - z - steps) % 8
            source = i % 2 * 4 + column

            @pl.when(jnp.logical_and(column < 4, source != dp))
            def _():
                arrived(parts_in.at[source], sum_r.at[source])
                largest = parts_in[source, height:, :].astype(F32)
                total[rows, :] += decode(parts_in[source, :height, :], largest[:1])

    def beside_g(step, j):
        if (step, j) == (2, 1):
            ring_start(blk_a, ring_a)
        if j == 1:
            rotate_g(2 * step - 1)
            rotate_g(2 * step)
        elif step == 3:
            rotate_g(7)

    def beside_a(step, j):
        if j == 1:
            if step == 1:
                rotate_a(0)
            rotate_a(2 * step - 1)
            rotate_a(2 * step)
        elif step == 3:
            rotate_a(7)

    grad_own, act_own = cols.at[dp, pl.ds(0, GRAD)], cols.at[dp, pl.ds(GRAD, ACT)]
    enter(grad_own, blk_g.at[dp, core, half], ring_g[0], ring_g[1])
    enter(act_own, blk_a.at[dp, core, half], ring_a[0], ring_a[1])
    column_copy(dp, opposite, opposite).start()
    loads[2].wait()
    bin_t[...] = bin_raw[...].T
    total[...] = jnp.zeros_like(total)
    ring_start(blk_g, ring_g)
    send_columns()
    loads[3].wait()
    rotate_g(0)
    ring_rest(blk_g, ring_g, beside_g)
    ring_rest(blk_a, ring_a, beside_a)

    def tokens(ref, *index):
        return jnp.concatenate([ref[(t,) + index] for t in range(GROUPS)], axis=1)

    grad_rows, act_rows = pl.ds(0, GRAD), pl.ds(GRAD, ACT)
    scale = 1.0 / (GROUPS * CHUNK)

    def covariance_out(j):
        rows = jnp.concatenate([tokens(blk_g, c, j) for c in range(2)], axis=0)
        cov_out[:, 2 * GRAD * j : 2 * GRAD * (j + 1)] = (
            dot_nt(tokens(cols, grad_rows), rows) * scale
        )

    def squares(rows):
        sums = total[rows, :] + mine[rows, :]
        return (sums * sums).astype(BF16)

    add_parts(slice(0, GRAD), in_g, sum_gr)
    gsq[dp] = squares(slice(0, GRAD))
    add_parts(slice(GRAD, BOTH), in_a, sum_ar)
    asq_own[...] = squares(slice(GRAD, BOTH))
    enter(asq_own, asq.at[dp, core, half], ring_q[0], ring_q[1])

    @pl.loop(1, GROUPS)
    def _(i):
        source = (dp + i) % 8

        @pl.when(source != opposite)
        def _():
            arrived(cols.at[source], col_r.at[source])

    covariance_out(0)
    covariance_out(1)

    def beside_q(step, j):
        if (step, j) == (2, 0):
            entered(grad_own, ring_g[0])
            entered(act_own, ring_a[0])
            ring_sent(blk_g, ring_g)
            ring_sent(blk_a, ring_a)

            @pl.loop(1, GROUPS)
            def _(i):
                peer = (dp + i) % 8
                sent(cols.at[dp], col_s.at[peer])
                sent(part_g.at[peer], sum_gs.at[peer])
                sent(part_a.at[peer], sum_as.at[peer])

    ring_start(asq, ring_q)

    @pl.loop(1, GROUPS)
    def _(i):
        peer = (dp + i) % 8
        remote(gsq.at[dp], gsq.at[dp], gsq_s.at[peer], gsq_r.at[dp], (peer, own)).start()

    rows = jnp.concatenate(
        [tokens(blk_a, c, j) for j in range(2) for c in range(2)], axis=0
    )
    cov_in[...] = dot_nt(rows, tokens(cols, act_rows)) * scale
    ring_rest(asq, ring_q, beside_q)

    @pl.loop(1, GROUPS)
    def _(i):
        source, peer = (dp + i) % 8, (dp + i) % 8
        arrived(gsq.at[source], gsq_r.at[source])
        sent(gsq.at[dp], gsq_s.at[peer])

    for index in range(8):
        shared(asq, ring_q, index)
    entered(asq_own, ring_q[0])
    ring_sent(asq, ring_q)


def finish(cov_out, cov_in, gsq, asq, cov_out_hbm, cov_in_hbm, corr_hbm, corr, sem):
    first = pltpu.make_async_copy(cov_out, cov_out_hbm, sem.at[0])
    second = pltpu.make_async_copy(cov_in, cov_in_hbm, sem.at[1])
    first.start()
    second.start()
    left = jnp.concatenate([gsq[t] for t in range(GROUPS)], axis=1)
    for j in range(2):
        right = jnp.concatenate(
            [
                jnp.concatenate([asq[t, c, j] for t in range(GROUPS)], axis=1)
                for c in range(2)
            ],
            axis=0,
        )
        columns = slice(2 * ACT * j, 2 * ACT * (j + 1))
        corr[:, columns] = dot_nt(left, right) * (1.0 / (GROUPS * CHUNK))
    last = pltpu.make_async_copy(corr, corr_hbm, sem.at[2])
    last.start()
    first.wait()
    second.wait()
    last.wait()


def on_device(gradients, activations, basis_out, basis_in):
    dma = pltpu.SemaphoreType.DMA
    ring_sems = [dma((2,))] * 4 + [dma((3, 2))] * 4 + [dma((8, 2))] * 2
    inputs = [
        pltpu.with_memory_space_constraint(x, pltpu.HBM)
        for x in (gradients.T, activations, basis_out.T, basis_in)
    ]
    results = pl.pallas_call(
        kernel,
        out_shape=(
            pltpu.VMEM((GRAD, 4 * GRAD), F32),
            pltpu.VMEM((4 * ACT, ACT), F32),
            pltpu.VMEM((GROUPS, GRAD, CHUNK), BF16),
            pltpu.VMEM((GROUPS, 2, 2, ACT, CHUNK), BF16),
        ),
        in_specs=[pl.BlockSpec(memory_space=pl.ANY)] * 4,
        out_specs=[pl.BlockSpec(memory_space=pltpu.VMEM)] * 4,
        scratch_shapes=[
            pltpu.VMEM((GROUPS, BOTH, CHUNK), BF16),
            pltpu.VMEM((GROUPS, 2, 2, GRAD, CHUNK), BF16),
            pltpu.VMEM((GROUPS, 2, 2, ACT, CHUNK), BF16),
            pltpu.VMEM((GRAD, 4 * GRAD), BF16),
            pltpu.VMEM((4 * ACT, ACT), BF16),
            pltpu.VMEM((ACT, 4 * ACT), BF16),
            pltpu.VMEM((CHUNK, ACT), BF16),
            pltpu.VMEM((BOTH, CHUNK), F32),
            pltpu.VMEM((GROUPS, GRAD + SCALES, CHUNK), BF16),
            pltpu.VMEM((GROUPS, ACT + SCALES, CHUNK), BF16),
            pltpu.VMEM((GROUPS, GRAD + SCALES, CHUNK), BF16),
            pltpu.VMEM((GROUPS, ACT + SCALES, CHUNK), BF16),
            pltpu.VMEM((BOTH, CHUNK), F32),
            pltpu.VMEM((BOTH, CHUNK), F32),
            pltpu.VMEM((ACT, CHUNK), BF16),
            dma((4,)),
            *ring_sems * 3,
            *[dma((GROUPS,))] * 8,
        ],
        compiler_params=pltpu.CompilerParams(
            collective_id=0, has_side_effects=True, vmem_limit_bytes=36 << 20
        ),
    )(*inputs)
    results = [pltpu.with_memory_space_constraint(x, pltpu.VMEM) for x in results]
    cov_out_t, cov_in, corrections = pl.pallas_call(
        finish,
        out_shape=(
            jax.ShapeDtypeStruct((GRAD, 4 * GRAD), F32),
            jax.ShapeDtypeStruct((4 * ACT, ACT), F32),
            jax.ShapeDtypeStruct((GRAD, 4 * ACT), F32),
        ),
        in_specs=[pl.BlockSpec(memory_space=pltpu.VMEM)] * 4,
        out_specs=[pl.BlockSpec(memory_space=pl.ANY)] * 3,
        scratch_shapes=[pltpu.VMEM((GRAD, 4 * ACT), F32), dma((3,))],
        compiler_params=pltpu.CompilerParams(vmem_limit_bytes=36 << 20),
    )(*results)
    return cov_out_t.T, cov_in, corrections


def solution(mesh):
    placed = (P("dp", "owner"), P("dp", "owner"), P("dp", "owner"), P("dp", "owner"))
    return jax.shard_map(
        on_device,
        mesh=mesh,
        in_specs=placed,
        out_specs=(P("dp", "owner"), P("dp", "owner"), P("owner", "dp")),
        check_vma=False,
    )
```

```python
import jax
import jax.numpy as jnp
from jax import lax
from jax.experimental import pallas as pl
from jax.experimental.pallas import tpu as pltpu
from jax.sharding import PartitionSpec as P

BF16, F32 = jnp.bfloat16, jnp.float32
MESH = pl.DeviceIdType.MESH
GROUPS = 8
CHUNK = 128
GRAD = 448
ACT = 256
BOTH = GRAD + ACT
SCALES = 16
SPAN = 240.0


def dot_nt(left, right):
    return lax.dot_general(
        left, right, (((1,), (1,)), ((), ())), preferred_element_type=F32
    )


def dot_nn(left, right):
    return lax.dot_general(
        left, right, (((1,), (0,)), ((), ())), preferred_element_type=F32
    )


def encode(values):
    largest = jnp.max(jnp.abs(values), axis=0, keepdims=True)
    scale = jnp.maximum(largest * 1.0079, 1e-30).astype(BF16).astype(F32)
    code = jnp.exp2(jnp.abs(values) * (SPAN / scale) - SPAN / 2)
    return jnp.where(values < 0, -code, code).astype(BF16), scale


def decode(code, scale):
    code = code.astype(F32)
    values = (jnp.log2(jnp.abs(code)) + SPAN / 2) * (scale * (1 / SPAN))
    return jnp.where(code < 0, -values, values)


def kernel(
    grad_hbm, act_hbm, bout_hbm, bin_hbm,
    cov_out, cov_in, gsq, asq,
    cols, blk_g, blk_a, bout, bin_raw, bin_t, act_raw, rot, part_g, part_a, in_g, in_a,
    mine, total, asq_own, load_sem, *sems,
):
    ring_g, ring_a, ring_q = sems[:10], sems[10:20], sems[20:30]
    col_s, col_r, sum_gs, sum_gr, sum_as, sum_ar, gsq_s, gsq_r = sems[30:]
    dp, own = lax.axis_index("dp"), lax.axis_index("owner")
    side, z, core = own // 16, (own // 2) % 8, own % 2
    sibling = own + 1 - 2 * core
    across = (own + 16) % 32
    up = side * 16 + ((z + 1) % 8) * 2 + core
    down = side * 16 + ((z + 7) % 8) * 2 + core

    def chunk_at(position):
        return (4 * side + 16 - position - dp % 4) % 8

    first = chunk_at(z)
    line = own // 4
    half = z % 2

    def entry(ring):
        return (4 * ring + 16 - dp - line % 4) % 8


    def remote(src, dst, send, recv, to):
        return pltpu.make_async_remote_copy(
            src_ref=src, dst_ref=dst, send_sem=send, recv_sem=recv,
            device_id=to, device_id_type=MESH,
        )

    def arrived(ref, recv):
        remote(ref, ref, load_sem.at[0], recv, (dp, sibling)).wait_recv()

    def sent(ref, send):
        remote(ref, ref, send, load_sem.at[0], (dp, sibling)).wait_send()

    loads = [
        pltpu.make_async_copy(act_hbm, act_raw, load_sem.at[0]),
        pltpu.make_async_copy(grad_hbm, cols.at[dp, pl.ds(0, GRAD)], load_sem.at[1]),
        pltpu.make_async_copy(bin_hbm, bin_raw, load_sem.at[2]),
        pltpu.make_async_copy(bout_hbm, bout, load_sem.at[3]),
    ]
    for load in loads:
        load.start()

    barrier = pltpu.get_barrier_semaphore()

    def greet(to):
        pl.semaphore_signal(barrier, inc=1, device_id=to, device_id_type=MESH)

    @pl.loop(1, GROUPS)
    def _(i):
        greet(((dp + i) % 8, own))

    greet((dp, sibling))
    greet((dp, across))
    greet((dp, up))
    greet((dp, down))
    for j in range(2):
        source = 4 * dp + 2 * j + core

        @pl.when(jnp.logical_or(first != dp, source != own))
        def _():
            greet((first, source))

    loads[1].wait()
    at_home = jnp.logical_and(line == dp, entry(side) == z)
    pl.semaphore_wait(barrier, 13 - jnp.where(at_home, 1, 0))

    def enter(src, dst, send, recv):
        for j in range(2):
            target = j * 16 + entry(j) * 2 + core
            local = jnp.logical_and(line == dp, target == own)

            @pl.when(local)
            def _():
                pltpu.make_async_copy(src, dst, recv.at[half]).start()

            @pl.when(jnp.logical_not(local))
            def _():
                remote(src, dst, send.at[j], recv.at[half], (line, target)).start()

    def entered(src, send):
        for j in range(2):
            target = j * 16 + entry(j) * 2 + core
            local = jnp.logical_and(line == dp, target == own)

            @pl.when(jnp.logical_not(local))
            def _():
                sent(src, send.at[j])

    def ring_copies(buf, ring):
        ent_s, ent_r, x_s, x_r, up_s, up_r, dn_s, dn_r, sib_s, sib_r = ring

        def share(index, j, ref):
            remote(
                ref, ref, sib_s.at[index, j], sib_r.at[index, j], (dp, sibling)
            ).start()

        def to_up(step, j, ref):
            remote(ref, ref, up_s.at[step, j], up_r.at[step, j], (dp, up)).start()

        def to_down(step, j, ref):
            remote(ref, ref, dn_s.at[step, j], dn_r.at[step, j], (dp, down)).start()

        return share, to_up, to_down

    def ring_start(buf, ring):
        share, to_up, to_down = ring_copies(buf, ring)
        for j in range(2):
            piece = buf.at[first, core, j]
            arrived(piece, ring[1].at[j])
            to_up(0, j, piece)
            to_down(0, j, piece)
            remote(piece, piece, ring[2].at[j], ring[3].at[j], (dp, across)).start()
            share(0, j, piece)

    def ring_rest(buf, ring, between, wide=False):
        share, to_up, to_down = ring_copies(buf, ring)

        def cross(index, ref):
            remote(ref, ref, ring[2].at[index], ring[3].at[index], (dp, across)).start()

        for step in range(1, 4):
            below, above = chunk_at(z - step), chunk_at(z + step)
            for j in range(2):
                piece = buf.at[below, core, j]
                crossed = wide and step == 3 and j == 1
                arrived(piece, ring[3].at[3] if crossed else ring[5].at[step - 1, j])
                if step == 1 or (step == 2 and not (wide and j)):
                    to_up(step, j, piece)
                if wide and step == 1 and j == 1:
                    cross(2, piece)
                share(2 * step - 1, j, piece)
                piece = buf.at[above, core, j]
                arrived(piece, ring[3].at[2] if crossed else ring[7].at[step - 1, j])
                if step == 1 or (step == 2 and not (wide and j)):
                    to_down(step, j, piece)
                if wide and step == 1 and j == 1:
                    cross(3, piece)
                share(2 * step, j, piece)
                if step == 2:
                    piece = buf.at[chunk_at(z + 4), core, j]
                    arrived(piece, ring[3].at[j])
                    share(7, j, piece)
                between(step, j)

    def shared(buf, ring, index):
        step = (index + 1) // 2
        chunk = chunk_at(z - step if index % 2 else z + step)
        for j in range(2):
            arrived(buf.at[chunk, 1 - core, j], ring[9].at[index, j])
        return chunk

    def ring_sent(buf, ring, wide=False):
        piece = buf.at[first, core, 0]
        for j in range(2):
            sent(piece, ring[2].at[j])
            if wide:
                sent(piece, ring[2].at[2 + j])
            for step in range(2 if wide and j else 3):
                sent(piece, ring[4].at[step, j])
                sent(piece, ring[6].at[step, j])
            for index in range(8):
                sent(piece, ring[8].at[index, j])

    def rotate(index, buf, ring, basis, rows, part, parts_in, sum_s, sum_r):
        t = shared(buf, ring, index)
        features = jnp.concatenate(
            [buf[t, c, j] for j in range(2) for c in range(2)], axis=0
        )
        rot[rows, :] = dot_nn(basis[...], features)
        height = rows.stop - rows.start

        @pl.when(t == dp)
        def _():
            mine[rows, :] = rot[rows, :]

        @pl.when(t != dp)
        def _():
            code, largest = encode(rot[rows, :])
            part[t, :height, :] = code
            part[t, height:, :] = jnp.broadcast_to(largest, (SCALES, CHUNK)).astype(BF16)
            remote(part.at[t], parts_in.at[dp], sum_s.at[t], sum_r.at[dp], (t, own)).start()

    def rotate_g(index):
        rotate(index, blk_g, ring_g, bout, slice(0, GRAD), part_g, in_g, sum_gs, sum_gr)

    def rotate_a(index):
        rotate(index, blk_a, ring_a, bin_t, slice(GRAD, BOTH), part_a, in_a, sum_as, sum_ar)

    opposite = (dp + 4) % 8

    def column_copy(chunk, index, peer):
        return remote(
            cols.at[chunk], cols.at[chunk], col_s.at[index], col_r.at[chunk], (peer, own)
        )

    def send_columns():
        arrived(cols.at[opposite], col_r.at[opposite])

        @pl.loop(1, 4)
        def _(i):
            peer = dp // 4 * 4 + (dp + i) % 4
            column_copy(opposite, (peer + 4) % 8, peer).start()

    def add_parts(rows, parts_in, sum_r, low, high):
        height = rows.stop - rows.start

        @pl.loop(2 * low, 2 * high)
        def _(i):
            turn = i // 2
            steps = (turn + 1) // 2 * (1 - 2 * (turn % 2))
            column = (4 * side + 24 - dp - z - steps) % 8
            source = i % 2 * 4 + column

            @pl.when(jnp.logical_and(column < 4, source != dp))
            def _():
                arrived(parts_in.at[source], sum_r.at[source])
                largest = parts_in[source, height:, :].astype(F32)
                total[rows, :] += decode(parts_in[source, :height, :], largest[:1])

    def beside_g(step, j):
        if (step, j) == (2, 1):
            ring_start(blk_a, ring_a)
        if j == 1:
            rotate_g(2 * step - 1)
            rotate_g(2 * step)
        elif step == 3:
            rotate_g(7)

    def beside_a(step, j):
        if j == 1:
            if step == 1:
                rotate_a(0)
            rotate_a(2 * step - 1)
            rotate_a(2 * step)
        elif step == 3:
            rotate_a(7)
            add_parts(slice(0, GRAD), in_g, sum_gr, 0, 3)

    grad_own, act_own = cols.at[dp, pl.ds(0, GRAD)], cols.at[dp, pl.ds(GRAD, ACT)]
    enter(grad_own, blk_g.at[dp, core, half], ring_g[0], ring_g[1])
    loads[0].wait()
    cols[dp, GRAD:, :] = act_raw[...].T
    enter(act_own, blk_a.at[dp, core, half], ring_a[0], ring_a[1])
    column_copy(dp, opposite, opposite).start()

    @pl.loop(1, 4)
    def _(i):
        peer = dp // 4 * 4 + (dp + i) % 4
        column_copy(dp, peer, peer).start()

    loads[2].wait()
    bin_t[...] = bin_raw[...].T
    total[...] = jnp.zeros_like(total)
    ring_start(blk_g, ring_g)
    send_columns()
    loads[3].wait()
    rotate_g(0)
    ring_rest(blk_g, ring_g, beside_g)
    ring_rest(blk_a, ring_a, beside_a)

    def tokens(ref, *index):
        return jnp.concatenate([ref[(t,) + index] for t in range(GROUPS)], axis=1)

    grad_rows, act_rows = pl.ds(0, GRAD), pl.ds(GRAD, ACT)
    scale = 1.0 / (GROUPS * CHUNK)

    def covariance_out(j):
        rows = jnp.concatenate([tokens(blk_g, c, j) for c in range(2)], axis=0)
        cov_out[:, 2 * GRAD * j : 2 * GRAD * (j + 1)] = (
            dot_nt(tokens(cols, grad_rows), rows) * scale
        )

    def squares(rows):
        sums = total[rows, :] + mine[rows, :]
        return (sums * sums).astype(BF16)

    add_parts(slice(GRAD, BOTH), in_a, sum_ar, 0, 8)
    asq_own[...] = squares(slice(GRAD, BOTH))
    enter(asq_own, asq.at[dp, core, half], ring_q[0], ring_q[1])
    add_parts(slice(0, GRAD), in_g, sum_gr, 3, 8)
    def square_copy(chunk, index, peer):
        return remote(
            gsq.at[chunk], gsq.at[chunk], gsq_s.at[index], gsq_r.at[chunk], (peer, own)
        )

    gsq[dp] = squares(slice(0, GRAD))
    square_copy(dp, opposite, opposite).start()


    def beside_q(step, j):
        if (step, j) == (1, 1):
            covariance_out(1)
        if (step, j) == (2, 0):
            entered(grad_own, ring_g[0])
            entered(act_own, ring_a[0])
            ring_sent(blk_g, ring_g)
            ring_sent(blk_a, ring_a)

            @pl.loop(1, GROUPS)
            def _(i):
                peer = (dp + i) % 8
                sent(cols.at[dp], col_s.at[peer])
                sent(part_g.at[peer], sum_gs.at[peer])
                sent(part_a.at[peer], sum_as.at[peer])

    ring_start(asq, ring_q)

    arrived(gsq.at[opposite], gsq_r.at[opposite])

    @pl.loop(1, 4)
    def _(i):
        peer = dp // 4 * 4 + (dp + i) % 4
        square_copy(dp, peer, peer).start()
        square_copy(opposite, (peer + 4) % 8, peer).start()

    @pl.loop(1, GROUPS)
    def _(i):
        source = (dp + i) % 8

        @pl.when(source != opposite)
        def _():
            arrived(cols.at[source], col_r.at[source])

    covariance_out(0)
    rows = jnp.concatenate(
        [tokens(blk_a, c, j) for j in range(2) for c in range(2)], axis=0
    )
    cov_in[...] = dot_nt(rows, tokens(cols, act_rows)) * scale
    ring_rest(asq, ring_q, beside_q)

    @pl.loop(1, GROUPS)
    def _(i):
        source, peer = (dp + i) % 8, (dp + i) % 8

        @pl.when(source != opposite)
        def _():
            arrived(gsq.at[source], gsq_r.at[source])

        sent(gsq.at[dp], gsq_s.at[peer])

    for index in range(8):
        shared(asq, ring_q, index)
    entered(asq_own, ring_q[0])
    ring_sent(asq, ring_q)


def finish(cov_out, cov_in, gsq, asq, cov_out_hbm, cov_in_hbm, corr_hbm, corr, sem):
    first = pltpu.make_async_copy(cov_out, cov_out_hbm, sem.at[0])
    second = pltpu.make_async_copy(cov_in, cov_in_hbm, sem.at[1])
    first.start()
    second.start()
    left = jnp.concatenate([gsq[t] for t in range(GROUPS)], axis=1)
    for j in range(2):
        right = jnp.concatenate(
            [
                jnp.concatenate([asq[t, c, j] for t in range(GROUPS)], axis=1)
                for c in range(2)
            ],
            axis=0,
        )
        columns = slice(2 * ACT * j, 2 * ACT * (j + 1))
        corr[:, columns] = dot_nt(left, right) * (1.0 / (GROUPS * CHUNK))
    last = pltpu.make_async_copy(corr, corr_hbm, sem.at[2])
    last.start()
    first.wait()
    second.wait()
    last.wait()


def on_device(gradients, activations, basis_out, basis_in):
    dma = pltpu.SemaphoreType.DMA
    ring_sems = [dma((2,))] * 2 + [dma((4,))] * 2 + [dma((3, 2))] * 4 + [dma((8, 2))] * 2
    inputs = [
        pltpu.with_memory_space_constraint(x, pltpu.HBM)
        for x in (gradients.T, activations, basis_out.T, basis_in)
    ]
    results = pl.pallas_call(
        kernel,
        out_shape=(
            pltpu.VMEM((GRAD, 4 * GRAD), F32),
            pltpu.VMEM((4 * ACT, ACT), F32),
            pltpu.VMEM((GROUPS, GRAD, CHUNK), BF16),
            pltpu.VMEM((GROUPS, 2, 2, ACT, CHUNK), BF16),
        ),
        in_specs=[pl.BlockSpec(memory_space=pl.ANY)] * 4,
        out_specs=[pl.BlockSpec(memory_space=pltpu.VMEM)] * 4,
        scratch_shapes=[
            pltpu.VMEM((GROUPS, BOTH, CHUNK), BF16),
            pltpu.VMEM((GROUPS, 2, 2, GRAD, CHUNK), BF16),
            pltpu.VMEM((GROUPS, 2, 2, ACT, CHUNK), BF16),
            pltpu.VMEM((GRAD, 4 * GRAD), BF16),
            pltpu.VMEM((4 * ACT, ACT), BF16),
            pltpu.VMEM((ACT, 4 * ACT), BF16),
            pltpu.VMEM((CHUNK, ACT), BF16),
            pltpu.VMEM((BOTH, CHUNK), F32),
            pltpu.VMEM((GROUPS, GRAD + SCALES, CHUNK), BF16),
            pltpu.VMEM((GROUPS, ACT + SCALES, CHUNK), BF16),
            pltpu.VMEM((GROUPS, GRAD + SCALES, CHUNK), BF16),
            pltpu.VMEM((GROUPS, ACT + SCALES, CHUNK), BF16),
            pltpu.VMEM((BOTH, CHUNK), F32),
            pltpu.VMEM((BOTH, CHUNK), F32),
            pltpu.VMEM((ACT, CHUNK), BF16),
            dma((4,)),
            *ring_sems * 3,
            *[dma((GROUPS,))] * 8,
        ],
        compiler_params=pltpu.CompilerParams(
            collective_id=0, has_side_effects=True, vmem_limit_bytes=36 << 20
        ),
    )(*inputs)
    results = [pltpu.with_memory_space_constraint(x, pltpu.VMEM) for x in results]
    cov_out_t, cov_in, corrections = pl.pallas_call(
        finish,
        out_shape=(
            jax.ShapeDtypeStruct((GRAD, 4 * GRAD), F32),
            jax.ShapeDtypeStruct((4 * ACT, ACT), F32),
            jax.ShapeDtypeStruct((GRAD, 4 * ACT), F32),
        ),
        in_specs=[pl.BlockSpec(memory_space=pltpu.VMEM)] * 4,
        out_specs=[pl.BlockSpec(memory_space=pl.ANY)] * 3,
        scratch_shapes=[pltpu.VMEM((GRAD, 4 * ACT), F32), dma((3,))],
        compiler_params=pltpu.CompilerParams(vmem_limit_bytes=36 << 20),
    )(*results)
    return cov_out_t.T, cov_in, corrections


def solution(mesh):
    placed = (P("dp", "owner"), P("dp", "owner"), P("dp", "owner"), P("dp", "owner"))
    return jax.shard_map(
        on_device,
        mesh=mesh,
        in_specs=placed,
        out_specs=(P("dp", "owner"), P("dp", "owner"), P("owner", "dp")),
        check_vma=False,
    )
```

```python
import jax
import jax.numpy as jnp
from jax import lax
from jax.experimental import pallas as pl
from jax.experimental.pallas import tpu as pltpu
from jax.sharding import PartitionSpec as P

BF16, F32 = jnp.bfloat16, jnp.float32
MESH = pl.DeviceIdType.MESH
GROUPS = 8
CHUNK = 128
GRAD = 448
ACT = 256
BOTH = GRAD + ACT
SCALES = 16
SPAN = 240.0


def dot_nt(left, right):
    return lax.dot_general(
        left, right, (((1,), (1,)), ((), ())), preferred_element_type=F32
    )


def dot_nn(left, right):
    return lax.dot_general(
        left, right, (((1,), (0,)), ((), ())), preferred_element_type=F32
    )


def encode(values):
    largest = jnp.max(jnp.abs(values), axis=0, keepdims=True)
    scale = jnp.maximum(largest * 1.0079, 1e-30).astype(BF16).astype(F32)
    code = jnp.exp2(jnp.abs(values) * (SPAN / scale) - SPAN / 2)
    return jnp.where(values < 0, -code, code).astype(BF16), scale


def decode(code, scale):
    code = code.astype(F32)
    values = (jnp.log2(jnp.abs(code)) + SPAN / 2) * (scale * (1 / SPAN))
    return jnp.where(code < 0, -values, values)


def kernel(
    grad_hbm, act_hbm, bout_hbm, bin_hbm,
    cov_out, cov_in, gsq, asq,
    cols, blk_g, blk_a, bout, bin_raw, bin_t, act_raw, rot, part_g, part_a, in_g, in_a,
    mine, total, asq_own, load_sem, *sems,
):
    ring_g, ring_a, ring_q = sems[:10], sems[10:20], sems[20:30]
    col_s, col_r, sum_gs, sum_gr, sum_as, sum_ar, gsq_s, gsq_r = sems[30:]
    dp, own = lax.axis_index("dp"), lax.axis_index("owner")
    side, z, core = own // 16, (own // 2) % 8, own % 2
    sibling = own + 1 - 2 * core
    across = (own + 16) % 32
    up = side * 16 + ((z + 1) % 8) * 2 + core
    down = side * 16 + ((z + 7) % 8) * 2 + core

    def chunk_at(position):
        return (4 * side + 16 - position - dp % 4) % 8

    first = chunk_at(z)
    line = own // 4
    half = z % 2

    def entry(ring):
        return (4 * ring + 16 - dp - line % 4) % 8


    def remote(src, dst, send, recv, to):
        return pltpu.make_async_remote_copy(
            src_ref=src, dst_ref=dst, send_sem=send, recv_sem=recv,
            device_id=to, device_id_type=MESH,
        )

    def arrived(ref, recv):
        remote(ref, ref, load_sem.at[0], recv, (dp, sibling)).wait_recv()

    def sent(ref, send):
        remote(ref, ref, send, load_sem.at[0], (dp, sibling)).wait_send()

    loads = [
        pltpu.make_async_copy(act_hbm, act_raw, load_sem.at[0]),
        pltpu.make_async_copy(grad_hbm, cols.at[dp, pl.ds(0, GRAD)], load_sem.at[1]),
        pltpu.make_async_copy(bin_hbm, bin_raw, load_sem.at[2]),
        pltpu.make_async_copy(bout_hbm, bout, load_sem.at[3]),
    ]
    for load in loads:
        load.start()

    barrier = pltpu.get_barrier_semaphore()

    def greet(to):
        pl.semaphore_signal(barrier, inc=1, device_id=to, device_id_type=MESH)

    @pl.loop(1, GROUPS)
    def _(i):
        greet(((dp + i) % 8, own))

    greet((dp, sibling))
    greet((dp, across))
    greet((dp, up))
    greet((dp, down))
    for j in range(2):
        source = 4 * dp + 2 * j + core

        @pl.when(jnp.logical_or(first != dp, source != own))
        def _():
            greet((first, source))

    loads[1].wait()
    at_home = jnp.logical_and(line == dp, entry(side) == z)
    pl.semaphore_wait(barrier, 13 - jnp.where(at_home, 1, 0))

    def enter(src, dst, send, recv):
        for j in range(2):
            target = j * 16 + entry(j) * 2 + core
            local = jnp.logical_and(line == dp, target == own)

            @pl.when(local)
            def _():
                pltpu.make_async_copy(src, dst, recv.at[half]).start()

            @pl.when(jnp.logical_not(local))
            def _():
                remote(src, dst, send.at[j], recv.at[half], (line, target)).start()

    def entered(src, send):
        for j in range(2):
            target = j * 16 + entry(j) * 2 + core
            local = jnp.logical_and(line == dp, target == own)

            @pl.when(jnp.logical_not(local))
            def _():
                sent(src, send.at[j])

    def ring_copies(buf, ring):
        ent_s, ent_r, x_s, x_r, up_s, up_r, dn_s, dn_r, sib_s, sib_r = ring

        def share(index, j, ref):
            remote(
                ref, ref, sib_s.at[index, j], sib_r.at[index, j], (dp, sibling)
            ).start()

        def to_up(step, j, ref):
            remote(ref, ref, up_s.at[step, j], up_r.at[step, j], (dp, up)).start()

        def to_down(step, j, ref):
            remote(ref, ref, dn_s.at[step, j], dn_r.at[step, j], (dp, down)).start()

        return share, to_up, to_down

    def ring_start(buf, ring):
        share, to_up, to_down = ring_copies(buf, ring)
        for j in range(2):
            piece = buf.at[first, core, j]
            arrived(piece, ring[1].at[j])
            to_up(0, j, piece)
            to_down(0, j, piece)
            remote(piece, piece, ring[2].at[j], ring[3].at[j], (dp, across)).start()
            share(0, j, piece)

    def ring_rest(buf, ring, between, wide=False):
        share, to_up, to_down = ring_copies(buf, ring)

        def cross(index, ref):
            remote(ref, ref, ring[2].at[index], ring[3].at[index], (dp, across)).start()

        for step in range(1, 4):
            below, above = chunk_at(z - step), chunk_at(z + step)
            for j in range(2):
                piece = buf.at[below, core, j]
                crossed = wide and step == 3 and j == 1
                arrived(piece, ring[3].at[3] if crossed else ring[5].at[step - 1, j])
                if step == 1 or (step == 2 and not (wide and j)):
                    to_up(step, j, piece)
                if wide and step == 1 and j == 1:
                    cross(2, piece)
                share(2 * step - 1, j, piece)
                piece = buf.at[above, core, j]
                arrived(piece, ring[3].at[2] if crossed else ring[7].at[step - 1, j])
                if step == 1 or (step == 2 and not (wide and j)):
                    to_down(step, j, piece)
                if wide and step == 1 and j == 1:
                    cross(3, piece)
                share(2 * step, j, piece)
                if step == 2:
                    piece = buf.at[chunk_at(z + 4), core, j]
                    arrived(piece, ring[3].at[j])
                    share(7, j, piece)
                between(step, j)

    def shared(buf, ring, index):
        step = (index + 1) // 2
        chunk = chunk_at(z - step if index % 2 else z + step)
        for j in range(2):
            arrived(buf.at[chunk, 1 - core, j], ring[9].at[index, j])
        return chunk

    def ring_sent(buf, ring, wide=False):
        piece = buf.at[first, core, 0]
        for j in range(2):
            sent(piece, ring[2].at[j])
            if wide:
                sent(piece, ring[2].at[2 + j])
            for step in range(2 if wide and j else 3):
                sent(piece, ring[4].at[step, j])
                sent(piece, ring[6].at[step, j])
            for index in range(8):
                sent(piece, ring[8].at[index, j])

    def rotate(index, buf, ring, basis, rows, part, parts_in, sum_s, sum_r):
        t = shared(buf, ring, index)
        features = jnp.concatenate(
            [buf[t, c, j] for j in range(2) for c in range(2)], axis=0
        )
        rot[rows, :] = dot_nn(basis[...], features)
        height = rows.stop - rows.start

        @pl.when(t == dp)
        def _():
            mine[rows, :] = rot[rows, :]

        @pl.when(t != dp)
        def _():
            code, largest = encode(rot[rows, :])
            part[t, :height, :] = code
            part[t, height:, :] = jnp.broadcast_to(largest, (SCALES, CHUNK)).astype(BF16)
            remote(part.at[t], parts_in.at[dp], sum_s.at[t], sum_r.at[dp], (t, own)).start()

    def rotate_g(index):
        rotate(index, blk_g, ring_g, bout, slice(0, GRAD), part_g, in_g, sum_gs, sum_gr)

    def rotate_a(index):
        rotate(index, blk_a, ring_a, bin_t, slice(GRAD, BOTH), part_a, in_a, sum_as, sum_ar)

    opposite = (dp + 4) % 8

    def column_copy(chunk, index, peer):
        return remote(
            cols.at[chunk], cols.at[chunk], col_s.at[index], col_r.at[chunk], (peer, own)
        )

    def send_columns():
        arrived(cols.at[opposite], col_r.at[opposite])

        @pl.loop(1, 4)
        def _(i):
            peer = dp // 4 * 4 + (dp + i) % 4
            column_copy(opposite, (peer + 4) % 8, peer).start()

    def add_parts(rows, parts_in, sum_r, low, high):
        height = rows.stop - rows.start

        @pl.loop(2 * low, 2 * high)
        def _(i):
            turn = i // 2
            steps = (turn + 1) // 2 * (1 - 2 * (turn % 2))
            column = (4 * side + 24 - dp - z - steps) % 8
            source = i % 2 * 4 + column

            @pl.when(jnp.logical_and(column < 4, source != dp))
            def _():
                arrived(parts_in.at[source], sum_r.at[source])
                largest = parts_in[source, height:, :].astype(F32)
                total[rows, :] += decode(parts_in[source, :height, :], largest[:1])

    def beside_g(step, j):
        if (step, j) == (2, 1):
            ring_start(blk_a, ring_a)
        if j == 1:
            rotate_g(2 * step - 1)
            rotate_g(2 * step)
        elif step == 3:
            rotate_g(7)

    def beside_a(step, j):
        if j == 1:
            if step == 1:
                rotate_a(0)
            rotate_a(2 * step - 1)
            rotate_a(2 * step)
        elif step == 3:
            rotate_a(7)
            add_parts(slice(0, GRAD), in_g, sum_gr, 0, 3)

    grad_own, act_own = cols.at[dp, pl.ds(0, GRAD)], cols.at[dp, pl.ds(GRAD, ACT)]
    enter(grad_own, blk_g.at[dp, core, half], ring_g[0], ring_g[1])
    loads[0].wait()
    cols[dp, GRAD:, :] = act_raw[...].T
    enter(act_own, blk_a.at[dp, core, half], ring_a[0], ring_a[1])
    column_copy(dp, opposite, opposite).start()

    @pl.loop(1, 4)
    def _(i):
        peer = dp // 4 * 4 + (dp + i) % 4
        column_copy(dp, peer, peer).start()

    loads[2].wait()
    bin_t[...] = bin_raw[...].T
    total[...] = jnp.zeros_like(total)
    ring_start(blk_g, ring_g)
    send_columns()
    loads[3].wait()
    rotate_g(0)
    ring_rest(blk_g, ring_g, beside_g)
    ring_rest(blk_a, ring_a, beside_a)

    def tokens(ref, *index):
        return jnp.concatenate([ref[(t,) + index] for t in range(GROUPS)], axis=1)

    grad_rows, act_rows = pl.ds(0, GRAD), pl.ds(GRAD, ACT)
    scale = 1.0 / (GROUPS * CHUNK)

    def covariance_out(j):
        rows = jnp.concatenate([tokens(blk_g, c, j) for c in range(2)], axis=0)
        cov_out[:, 2 * GRAD * j : 2 * GRAD * (j + 1)] = (
            dot_nt(tokens(cols, grad_rows), rows) * scale
        )

    def squares(rows):
        sums = total[rows, :] + mine[rows, :]
        return (sums * sums).astype(BF16)

    add_parts(slice(GRAD, BOTH), in_a, sum_ar, 0, 8)
    asq_own[...] = squares(slice(GRAD, BOTH))
    enter(asq_own, asq.at[dp, core, half], ring_q[0], ring_q[1])
    add_parts(slice(0, GRAD), in_g, sum_gr, 3, 8)
    def square_copy(chunk, index, peer):
        return remote(
            gsq.at[chunk], gsq.at[chunk], gsq_s.at[index], gsq_r.at[chunk], (peer, own)
        )

    gsq[dp] = squares(slice(0, GRAD))
    square_copy(dp, opposite, opposite).start()


    def beside_q(step, j):
        if (step, j) == (1, 1):
            covariance_out(1)
        if (step, j) == (2, 0):
            entered(grad_own, ring_g[0])
            entered(act_own, ring_a[0])
            ring_sent(blk_g, ring_g)
            ring_sent(blk_a, ring_a)

            @pl.loop(1, GROUPS)
            def _(i):
                peer = (dp + i) % 8
                sent(cols.at[dp], col_s.at[peer])
                sent(part_g.at[peer], sum_gs.at[peer])
                sent(part_a.at[peer], sum_as.at[peer])

    ring_start(asq, ring_q)

    arrived(gsq.at[opposite], gsq_r.at[opposite])

    @pl.loop(1, 4)
    def _(i):
        peer = dp // 4 * 4 + (dp + i) % 4
        square_copy(dp, peer, peer).start()
        square_copy(opposite, (peer + 4) % 8, peer).start()

    @pl.loop(1, GROUPS)
    def _(i):
        source = (dp + i) % 8

        @pl.when(source != opposite)
        def _():
            arrived(cols.at[source], col_r.at[source])

    covariance_out(0)
    rows = jnp.concatenate(
        [tokens(blk_a, c, j) for j in range(2) for c in range(2)], axis=0
    )
    cov_in[...] = dot_nt(rows, tokens(cols, act_rows)) * scale
    ring_rest(asq, ring_q, beside_q)

    @pl.loop(1, GROUPS)
    def _(i):
        source, peer = (dp + i) % 8, (dp + i) % 8

        @pl.when(source != opposite)
        def _():
            arrived(gsq.at[source], gsq_r.at[source])

        sent(gsq.at[dp], gsq_s.at[peer])

    for index in range(8):
        shared(asq, ring_q, index)
    entered(asq_own, ring_q[0])
    ring_sent(asq, ring_q)


def finish(cov_out, cov_in, gsq, asq, cov_out_hbm, cov_in_hbm, corr_hbm, corr, sem):
    first = pltpu.make_async_copy(cov_out, cov_out_hbm, sem.at[0])
    second = pltpu.make_async_copy(cov_in, cov_in_hbm, sem.at[1])
    first.start()
    second.start()
    writes = [first, second]
    left = jnp.concatenate([gsq[t] for t in range(GROUPS)], axis=1)
    for j in range(2):
        right = jnp.concatenate(
            [
                jnp.concatenate([asq[t, c, j] for t in range(GROUPS)], axis=1)
                for c in range(2)
            ],
            axis=0,
        )
        columns = slice(2 * ACT * j, 2 * ACT * (j + 1))
        corr[:, columns] = dot_nt(left, right) * (1.0 / (GROUPS * CHUNK))
        part = pl.ds(2 * ACT * j, 2 * ACT)
        writes.append(
            pltpu.make_async_copy(corr.at[:, part], corr_hbm.at[:, part], sem.at[2 + j])
        )
        writes[-1].start()
    for write in writes:
        write.wait()


def on_device(gradients, activations, basis_out, basis_in):
    dma = pltpu.SemaphoreType.DMA
    ring_sems = [dma((2,))] * 2 + [dma((4,))] * 2 + [dma((3, 2))] * 4 + [dma((8, 2))] * 2
    inputs = [
        pltpu.with_memory_space_constraint(x, pltpu.HBM)
        for x in (gradients.T, activations, basis_out.T, basis_in)
    ]
    results = pl.pallas_call(
        kernel,
        out_shape=(
            pltpu.VMEM((GRAD, 4 * GRAD), F32),
            pltpu.VMEM((4 * ACT, ACT), F32),
            pltpu.VMEM((GROUPS, GRAD, CHUNK), BF16),
            pltpu.VMEM((GROUPS, 2, 2, ACT, CHUNK), BF16),
        ),
        in_specs=[pl.BlockSpec(memory_space=pl.ANY)] * 4,
        out_specs=[pl.BlockSpec(memory_space=pltpu.VMEM)] * 4,
        scratch_shapes=[
            pltpu.VMEM((GROUPS, BOTH, CHUNK), BF16),
            pltpu.VMEM((GROUPS, 2, 2, GRAD, CHUNK), BF16),
            pltpu.VMEM((GROUPS, 2, 2, ACT, CHUNK), BF16),
            pltpu.VMEM((GRAD, 4 * GRAD), BF16),
            pltpu.VMEM((4 * ACT, ACT), BF16),
            pltpu.VMEM((ACT, 4 * ACT), BF16),
            pltpu.VMEM((CHUNK, ACT), BF16),
            pltpu.VMEM((BOTH, CHUNK), F32),
            pltpu.VMEM((GROUPS, GRAD + SCALES, CHUNK), BF16),
            pltpu.VMEM((GROUPS, ACT + SCALES, CHUNK), BF16),
            pltpu.VMEM((GROUPS, GRAD + SCALES, CHUNK), BF16),
            pltpu.VMEM((GROUPS, ACT + SCALES, CHUNK), BF16),
            pltpu.VMEM((BOTH, CHUNK), F32),
            pltpu.VMEM((BOTH, CHUNK), F32),
            pltpu.VMEM((ACT, CHUNK), BF16),
            dma((4,)),
            *ring_sems * 3,
            *[dma((GROUPS,))] * 8,
        ],
        compiler_params=pltpu.CompilerParams(
            collective_id=0, has_side_effects=True, vmem_limit_bytes=36 << 20
        ),
    )(*inputs)
    results = [pltpu.with_memory_space_constraint(x, pltpu.VMEM) for x in results]
    cov_out_t, cov_in, corrections = pl.pallas_call(
        finish,
        out_shape=(
            jax.ShapeDtypeStruct((GRAD, 4 * GRAD), F32),
            jax.ShapeDtypeStruct((4 * ACT, ACT), F32),
            jax.ShapeDtypeStruct((GRAD, 4 * ACT), F32),
        ),
        in_specs=[pl.BlockSpec(memory_space=pltpu.VMEM)] * 4,
        out_specs=[pl.BlockSpec(memory_space=pl.ANY)] * 3,
        scratch_shapes=[pltpu.VMEM((GRAD, 4 * ACT), F32), dma((4,))],
        compiler_params=pltpu.CompilerParams(vmem_limit_bytes=36 << 20),
    )(*results)
    return cov_out_t.T, cov_in, corrections


def solution(mesh):
    placed = (P("dp", "owner"), P("dp", "owner"), P("dp", "owner"), P("dp", "owner"))
    return jax.shard_map(
        on_device,
        mesh=mesh,
        in_specs=placed,
        out_specs=(P("dp", "owner"), P("dp", "owner"), P("owner", "dp")),
        check_vma=False,
    )
```
